32 devices in a mesh: dp: 2 (over y), ctx: 16 (over z, x, core).
Axes of the slice: x: 2, y: 2, z: 4, core: 2. Of those that a mesh axis runs over, the one named last changes fastest.
Arguments:
- queries: bfloat16 [2, 2048, 1024], P('dp', 'ctx'), may hold values from -6 to 6
- keys: bfloat16 [2, 2048, 1024], P('dp', 'ctx'), may hold values from -0.5390625 to 0.5390625
- values: bfloat16 [2, 2048, 1024], P('dp', 'ctx'), may hold values from -6 to 6
- gain: float32 [1024], replicated, may hold values from 0.1 to 1.9
- grad_out: bfloat16 [2, 2048, 1024], P('dp', 'ctx'), may hold values from -16 to 16
Outputs:
- output: bfloat16 [2, 2048, 1024], P('dp', 'ctx')
- grad_queries: bfloat16 [2, 2048, 1024], P('dp', 'ctx')
- grad_keys: bfloat16 [2, 2048, 1024], P('dp', 'ctx')
- grad_values: bfloat16 [2, 2048, 1024], P('dp', 'ctx')
- grad_gain: float32 [1024], replicated
The draws below stay inside these ranges and needn't reach their ends.
All inputs are finite; a program needn't handle non-finite values.
Results may differ from the reference program's by a relative error of at most 0.006.
Values sent between devices are 32-bit elements; how exact they have to be, the bound alone decides.
A program may use at most 128 MiB of HBM per device.

```python
import jax
import jax.numpy as jnp
from jax import lax

HEADS = 16
HEAD_DIM = 64
GROUP = 128
WIDTH = 1024
SEQS = 2
LENGTH = 2048


def draw_grad_out(key, part):
    position = jnp.arange(LENGTH, dtype=jnp.float32) / (LENGTH - 1)
    base = jax.random.truncated_normal(key, -4.0, 4.0, (SEQS, LENGTH, WIDTH), jnp.float32)
    factor = 1.0 + 2.0 * position
    return (base * factor[None, :, None]).astype(jnp.bfloat16)


def levels(own_key, dims, shards, low, largest):
    level = 1.0
    for dim, blocks in shards:
        draws = jax.random.uniform(jax.random.fold_in(jax.random.fold_in(own_key, 6), dim), (blocks,), jnp.float32, low / len(shards), largest / len(shards))
        level = level * jnp.repeat(jnp.exp(draws), dims[dim] // blocks).reshape((-1,) + (1,) * (len(dims) - 1 - dim))
    return level


def noise(key, extent, deviation, bound, split=(), kind=jnp.bfloat16):
    factor_of = levels(key, extent, split, -0.22, 0.18) if split else 1.0
    entries = jax.random.normal(key, extent, jnp.float32) * deviation * factor_of
    return jnp.minimum(jnp.maximum(entries, -bound), bound).astype(kind)


def setup_inputs(seed: int = 0) -> dict:
    splits = jax.random.split(jax.random.key(seed), 6)
    return {
        "queries": noise(splits[0], (SEQS, LENGTH, WIDTH), 1.0, 6.0, ((0, 2), (1, 16))),
        "keys": noise(splits[1], (SEQS, LENGTH, WIDTH), 0.09, 0.5390625, ((0, 2), (1, 16))),
        "values": noise(splits[2], (SEQS, LENGTH, WIDTH), 1.0, 6.0, ((0, 2), (1, 16))),
        "gain": jnp.clip(1.0 + 0.18 * jax.random.normal(splits[3], (WIDTH,), jnp.float32), 0.1, 1.9),
        "grad_out": draw_grad_out(jax.random.fold_in(splits[5], 71), 0),
    }


def one_sequence(args, gain):
    queries, keys, values, grad_out = args
    blocks = LENGTH // GROUP
    shape4 = (blocks, GROUP, HEADS, HEAD_DIM)
    query_f = queries.reshape(shape4).astype(jnp.float32)
    key_f = keys.reshape(shape4).astype(jnp.float32)
    value_f = values.reshape(shape4).astype(jnp.float32)
    key_value = jnp.einsum('nrhd,nrhe->nhde', key_f, value_f)
    zeros = jnp.zeros((1, HEADS, HEAD_DIM, HEAD_DIM), jnp.float32)
    state = jnp.concatenate([zeros, jnp.cumsum(key_value, 0)[:-1]], 0)
    state_low = state.astype(jnp.bfloat16).astype(jnp.float32)
    causal = jnp.tril(jnp.ones((GROUP, GROUP), bool))
    scores = jnp.where(causal, jnp.einsum('nthd,nshd->nhts', query_f, key_f), 0.0).astype(jnp.bfloat16).astype(jnp.float32)
    attn = jnp.einsum('nhts,nshe->nthe', scores, value_f) + jnp.einsum('nthd,nhde->nthe', query_f, state_low)
    attn = attn.reshape(LENGTH, WIDTH)
    inverse_rms = lax.rsqrt(lax.optimization_barrier(jnp.mean(attn * attn, -1, keepdims=True)) + 1e-06)
    normed = attn * inverse_rms
    output = (normed * gain).astype(jnp.bfloat16)
    grad_f = grad_out.astype(jnp.float32)
    gain_part = lax.optimization_barrier(jnp.sum(grad_f * normed, 0))
    grad_norm = grad_f * gain
    grad_attn = (inverse_rms * (grad_norm - normed * lax.optimization_barrier(jnp.mean(grad_norm * normed, -1, keepdims=True)))).astype(jnp.bfloat16)
    grad_attn = grad_attn.reshape(shape4).astype(jnp.float32)
    query_grad = jnp.einsum('nthd,nthe->nhde', query_f, grad_attn)
    from_end = jnp.cumsum(query_grad[::-1], 0)[::-1]
    later = jnp.concatenate([from_end[1:], zeros], 0)
    later_low = later.astype(jnp.bfloat16).astype(jnp.float32)
    dscores = jnp.where(causal, jnp.einsum('nthe,nshe->nhts', grad_attn, value_f), 0.0).astype(jnp.bfloat16).astype(jnp.float32)
    grad_queries = jnp.einsum('nhts,nshd->nthd', dscores, key_f) + jnp.einsum('nthe,nhde->nthd', grad_attn, state_low)
    grad_keys = jnp.einsum('nhts,nthd->nshd', dscores, query_f) + jnp.einsum('nshe,nhde->nshd', value_f, later_low)
    grad_values = jnp.einsum('nhts,nthe->nshe', scores, grad_attn) + jnp.einsum('nshd,nhde->nshe', key_f, later_low)
    flat = (LENGTH, WIDTH)
    return (output, grad_queries.reshape(flat).astype(jnp.bfloat16), grad_keys.reshape(flat).astype(jnp.bfloat16), grad_values.reshape(flat).astype(jnp.bfloat16), gain_part)

def reference(queries, keys, values, gain, grad_out):
    results = lax.map(lambda a: one_sequence(a, gain), (queries, keys, values, grad_out))
    return (results[0], results[1], results[2], results[3], lax.optimization_barrier(jnp.sum(results[4], 0)))
```

```python
import functools

import jax
import jax.numpy as jnp
from jax import lax
from jax.experimental import pallas as pl
from jax.experimental.pallas import tpu as pltpu
from jax.sharding import PartitionSpec as P

HEAD_DIM = 64
GROUP = 128
LANES = 2 * HEAD_DIM
F32 = jnp.float32
BF16 = jnp.bfloat16
MESH = pl.DeviceIdType.MESH


def nn(a, b):
    return lax.dot_general(a, b, (((1,), (0,)), ((), ())), preferred_element_type=F32)


def nt(a, b):
    return lax.dot_general(a, b, (((1,), (1,)), ((), ())), preferred_element_type=F32)


def tn(a, b):
    return lax.dot_general(a, b, (((0,), (0,)), ((), ())), preferred_element_type=F32)


def first_head(rows):
    return lax.broadcasted_iota(jnp.int32, (rows, LANES), 1) < HEAD_DIM


def by_head(x):
    mask = first_head(x.shape[0])
    zero = jnp.zeros_like(x)
    return jnp.concatenate([jnp.where(mask, x, zero), jnp.where(mask, zero, x)], 0)


def pack(square):
    mask = first_head(HEAD_DIM)
    return jnp.where(mask, square[:HEAD_DIM], square[HEAD_DIM:])


def unpack(packed):
    mask = first_head(HEAD_DIM)
    zero = jnp.zeros_like(packed)
    both = [jnp.where(mask, packed, zero), jnp.where(mask, zero, packed)]
    return jnp.concatenate(both, 0).astype(BF16)


def side_by_side(stacked):
    return jnp.concatenate([stacked[:GROUP], stacked[GROUP:]], 1)


def kernel(
    n, ndp, q_hbm, k_hbm, v_hbm, gain_ref, g_hbm,
    out_hbm, gq_hbm, gk_hbm, gv_hbm, gg_ref,
    q, k, v, g, o_out, gq_out, gk_out, gv_out,
    attn, grad_attn, scores, gk_part, gv_part,
    kv, kv_in, prefix, state, qd, qd_in, suffix, later, gains,
    in_sems, out_sems, send_sems, recv_sems, gain_send, gain_recv,
):
    me = lax.axis_index("ctx")
    row = lax.axis_index("dp")
    width = q.shape[1]
    pairs = width // LANES
    share = kv.shape[1]
    slots = HEAD_DIM // share

    barrier = pltpu.get_barrier_semaphore()
    loads = []
    for i, (src, dst) in enumerate(((k_hbm, k), (v_hbm, v), (q_hbm, q), (g_hbm, g))):
        loads.append(pltpu.make_async_copy(src.at[0], dst, in_sems.at[i]))
        loads[-1].start()
    for hop in range(1, n):
        pl.semaphore_signal(
            barrier, inc=1, device_id={"ctx": lax.rem(me + hop, n)}, device_id_type=MESH
        )
    for hop in range(1, ndp):
        pl.semaphore_signal(
            barrier, inc=1, device_id={"dp": lax.rem(row + hop, ndp)}, device_id_type=MESH
        )

    def scatter(phase, source, target):
        for hop in range(1, n):
            peer = lax.rem(me + hop, n)
            pltpu.make_async_remote_copy(
                src_ref=source.at[peer],
                dst_ref=target.at[me],
                send_sem=send_sems.at[phase],
                recv_sem=recv_sems.at[phase],
                device_id={"ctx": peer},
                device_id_type=MESH,
            ).start()
        target[me] = source[me]

    def landed(phase, target):
        rest = target.at[pl.ds(0, n - 1)]
        pltpu.make_async_copy(rest, rest, recv_sems.at[phase]).wait()

    def left(phase, source):
        rest = source.at[pl.ds(0, n - 1)]
        pltpu.make_async_copy(rest, rest, send_sems.at[phase]).wait()

    def lanes(p):
        return slice(p * LANES, (p + 1) * LANES)

    def pair_of(ref, p):
        return ref[p * slots : (p + 1) * slots].reshape(HEAD_DIM, LANES)

    loads[0].wait()
    loads[1].wait()
    for p in range(pairs):
        packed = pack(tn(k[:, lanes(p)], v[:, lanes(p)]))
        kv[p * slots : (p + 1) * slots] = packed.reshape(slots, share, LANES)
    pl.semaphore_wait(barrier, n - 1 + ndp - 1)
    scatter(0, kv, kv_in)

    loads[2].wait()
    t = lax.broadcasted_iota(jnp.int32, (2 * GROUP, GROUP), 0) % GROUP
    causal = t >= lax.broadcasted_iota(jnp.int32, (2 * GROUP, GROUP), 1)

    def within(p):
        s = jnp.where(causal, nt(by_head(q[:, lanes(p)]), k[:, lanes(p)]), 0.0).astype(BF16)
        scores[p] = s
        attn[:, lanes(p)] = nn(side_by_side(s), by_head(v[:, lanes(p)]))

    for p in range(pairs // 2):
        within(p)

    landed(0, kv_in)
    total = jnp.zeros((share, LANES), F32)
    for j in range(n):
        prefix[j] = total
        total = total + kv_in[j]
    scatter(1, prefix, state)
    for p in range(pairs // 2, pairs):
        within(p)
    loads[3].wait()
    landed(1, state)

    squares = jnp.zeros((GROUP, LANES), F32)
    cross = jnp.zeros((GROUP, LANES), F32)
    for p in range(pairs):
        a = attn[:, lanes(p)] + nn(q[:, lanes(p)], unpack(pair_of(state, p)))
        attn[:, lanes(p)] = a
        squares += a * a
        cross += a * (g[:, lanes(p)].astype(F32) * gain_ref[:, lanes(p)])
    inv = lax.rsqrt(jnp.sum(squares, 1, keepdims=True) / width + 1e-06)
    mean = jnp.sum(cross, 1, keepdims=True) * inv / width
    gain_rows = []
    for p in range(pairs):
        normed = attn[:, lanes(p)] * inv
        gf = g[:, lanes(p)].astype(F32)
        ga = (inv * (gf * gain_ref[:, lanes(p)] - normed * mean)).astype(BF16)
        grad_attn[:, lanes(p)] = ga
        packed = pack(tn(q[:, lanes(p)], ga))
        qd[p * slots : (p + 1) * slots, :share] = packed.reshape(slots, share, LANES)
        gain_rows.append(jnp.sum(gf * normed, 0, keepdims=True))
    gain_tile = jnp.concatenate(gain_rows, 0)
    for j in range(n):
        qd[j, share:] = gain_tile
    scatter(2, qd, qd_in)

    def after(p):
        normed = attn[:, lanes(p)] * inv
        o_out[:, lanes(p)] = (normed * gain_ref[:, lanes(p)]).astype(BF16)
        ga = grad_attn[:, lanes(p)]
        ga2 = by_head(ga)
        ds = jnp.where(causal, nt(ga2, v[:, lanes(p)]), 0.0).astype(BF16)
        gq = nn(side_by_side(ds), by_head(k[:, lanes(p)]))
        gq = gq + nt(ga, unpack(pair_of(state, p)))
        gq_out[:, lanes(p)] = gq.astype(BF16)
        gk_part[:, lanes(p)] = tn(ds, by_head(q[:, lanes(p)]))
        gv_part[:, lanes(p)] = tn(scores[p], ga2)

    for p in range(pairs // 2):
        after(p)

    landed(2, qd_in)
    total = jnp.zeros((share, LANES), F32)
    for j in range(n - 1, -1, -1):
        suffix[j] = total
        total = total + qd_in[j, :share]
    scatter(3, suffix, later)
    gain_sum = qd_in[0, share:]
    for j in range(1, n):
        gain_sum = gain_sum + qd_in[j, share:]
    gains[row] = gain_sum
    for hop in range(1, ndp):
        pltpu.make_async_remote_copy(
            src_ref=gains.at[row],
            dst_ref=gains.at[row],
            send_sem=gain_send,
            recv_sem=gain_recv,
            device_id={"dp": lax.rem(row + hop, ndp)},
            device_id_type=MESH,
        ).start()
    for p in range(pairs // 2, pairs):
        after(p)
    stores = []

    def store(src, dst):
        stores.append(pltpu.make_async_copy(src, dst.at[0], out_sems.at[len(stores)]))
        stores[-1].start()

    store(o_out, out_hbm)
    store(gq_out, gq_hbm)

    landed(3, later)
    for p in range(pairs):
        low = unpack(pair_of(later, p))
        gk_out[:, lanes(p)] = (gk_part[:, lanes(p)] + nt(v[:, lanes(p)], low)).astype(BF16)
        gv_out[:, lanes(p)] = (gv_part[:, lanes(p)] + nn(k[:, lanes(p)], low)).astype(BF16)
    store(gk_out, gk_hbm)
    store(gv_out, gv_hbm)

    if ndp > 1:
        rest = gains.at[pl.ds(0, ndp - 1)]
        pltpu.make_async_copy(rest, rest, gain_recv).wait()
    gain_sum = gains[0]
    for j in range(1, ndp):
        gain_sum = gain_sum + gains[j]
    gg_ref[...] = gain_sum
    if ndp > 1:
        pltpu.make_async_copy(rest, rest, gain_send).wait()
    left(0, kv)
    left(1, prefix)
    left(2, qd)
    left(3, suffix)
    for copy in stores:
        copy.wait()


def per_device(n, ndp, queries, keys, values, gain, grad_out):
    rows, width = queries.shape[1:]
    pairs = width // LANES
    share = pairs * HEAD_DIM // n
    gain_rows = width // LANES
    flat = jax.ShapeDtypeStruct((1, rows, width), BF16)
    hbm = pl.BlockSpec(memory_space=pl.ANY)
    vmem = pl.BlockSpec(memory_space=pltpu.VMEM)
    low = pltpu.VMEM((rows, width), BF16)
    full = pltpu.VMEM((rows, width), F32)
    part = pltpu.VMEM((n, share, LANES), F32)
    wide = pltpu.VMEM((n, share + gain_rows, LANES), F32)
    dma = pltpu.SemaphoreType.DMA
    out, gq, gk, gv, gg = pl.pallas_call(
        functools.partial(kernel, n, ndp),
        out_shape=[flat] * 4 + [jax.ShapeDtypeStruct((gain_rows, LANES), F32)],
        in_specs=[hbm, hbm, hbm, vmem, hbm],
        out_specs=[hbm] * 4 + [vmem],
        scratch_shapes=[low] * 8
        + [full, low, pltpu.VMEM((pairs, 2 * GROUP, GROUP), BF16), full, full]
        + [part] * 4
        + [wide, wide, part, part, pltpu.VMEM((ndp, gain_rows, LANES), F32)]
        + [dma((4,)), dma((4,)), dma((4,)), dma((4,)), dma, dma],
        compiler_params=pltpu.CompilerParams(
            collective_id=0, has_side_effects=True, vmem_limit_bytes=48 * 2**20
        ),
        name="linear_attention",
    )(queries, keys, values, gain.reshape(1, width), grad_out)
    return out, gq, gk, gv, gg.reshape(width)


def solution(mesh):
    spec = P("dp", "ctx", None)
    return jax.shard_map(
        functools.partial(per_device, mesh.shape["ctx"], mesh.shape["dp"]),
        mesh=mesh,
        in_specs=(spec, spec, spec, P(), spec),
        out_specs=(spec, spec, spec, spec, P()),
        check_vma=False,
    )
```

```python
import functools

import jax
import jax.numpy as jnp
from jax import lax
from jax.experimental import pallas as pl
from jax.experimental.pallas import tpu as pltpu
from jax.sharding import PartitionSpec as P

HEAD_DIM = 64
GROUP = 128
LANES = 2 * HEAD_DIM
F32 = jnp.float32
BF16 = jnp.bfloat16
MESH = pl.DeviceIdType.MESH


def nn(a, b):
    return lax.dot_general(a, b, (((1,), (0,)), ((), ())), preferred_element_type=F32)


def nt(a, b):
    return lax.dot_general(a, b, (((1,), (1,)), ((), ())), preferred_element_type=F32)


def tn(a, b):
    return lax.dot_general(a, b, (((0,), (0,)), ((), ())), preferred_element_type=F32)


def first_head(rows):
    return lax.broadcasted_iota(jnp.int32, (rows, LANES), 1) < HEAD_DIM


def by_head(x):
    mask = first_head(x.shape[0])
    zero = jnp.zeros_like(x)
    return jnp.concatenate([jnp.where(mask, x, zero), jnp.where(mask, zero, x)], 0)


def pack(square):
    mask = first_head(HEAD_DIM)
    return jnp.where(mask, square[:HEAD_DIM], square[HEAD_DIM:])


def unpack(packed):
    mask = first_head(HEAD_DIM)
    zero = jnp.zeros_like(packed)
    both = [jnp.where(mask, packed, zero), jnp.where(mask, zero, packed)]
    return jnp.concatenate(both, 0).astype(BF16)


def side_by_side(stacked):
    return jnp.concatenate([stacked[:GROUP], stacked[GROUP:]], 1)


def scan_kernel(
    n, ndp, q_hbm, k_hbm, v_hbm, gain_hbm, g_hbm,
    k, v, o_out, gq_out, gk_part, gv_part, later, gg_ref,
    q, g, gain_ref, attn, grad_attn, scores,
    kv, kv_in, prefix, state, qd, qd_in, suffix, sums, carry, gains,
    in_sems, send_sems, recv_sems, carry_send, carry_recv, gain_send, gain_recv,
):
    me = lax.axis_index("ctx")
    row = lax.axis_index("dp")
    width = q.shape[1]
    pairs = width // LANES
    share = kv.shape[1]
    slots = HEAD_DIM // share
    half = n // 2
    upper = me // half
    place = lax.rem(me, half)
    other = lax.rem(me + half, n)

    barrier = pltpu.get_barrier_semaphore()
    loads = []
    arrays = (k_hbm.at[0], k), (v_hbm.at[0], v), (q_hbm.at[0], q), (g_hbm.at[0], g)
    for i, (src, dst) in enumerate(arrays + ((gain_hbm, gain_ref),)):
        loads.append(pltpu.make_async_copy(src, dst, in_sems.at[i]))
        loads[-1].start()

    mates = [lax.rem(place + hop, half) for hop in range(1, half)]
    twins = [(lax.rem(row + d, ndp), c) for d in range(ndp) for c in (me, other)][1:]
    for mate in mates:
        pl.semaphore_signal(
            barrier, inc=1, device_id={"ctx": upper * half + mate}, device_id_type=MESH
        )
    for d, c in twins:
        pl.semaphore_signal(barrier, inc=1, device_id={"dp": d, "ctx": c}, device_id_type=MESH)

    def scatter(phase, source, target):
        for mate in mates:
            pltpu.make_async_remote_copy(
                src_ref=source.at[mate],
                dst_ref=target.at[place],
                send_sem=send_sems.at[phase],
                recv_sem=recv_sems.at[phase],
                device_id={"ctx": upper * half + mate},
                device_id_type=MESH,
            ).start()
        target[place] = source[place]

    def landed(phase, target):
        rest = target.at[pl.ds(0, half - 1)]
        pltpu.make_async_copy(rest, rest, recv_sems.at[phase]).wait()

    def left(phase, source):
        rest = source.at[pl.ds(0, half - 1)]
        pltpu.make_async_copy(rest, rest, send_sems.at[phase]).wait()

    def carry_copy(way):
        return pltpu.make_async_remote_copy(
            src_ref=sums.at[way],
            dst_ref=carry.at[way],
            send_sem=carry_send.at[way],
            recv_sem=carry_recv.at[way],
            device_id={"ctx": other},
            device_id_type=MESH,
        )

    def cross(way, arrived, giver):
        sums[way] = functools.reduce(jnp.add, [arrived[j, :share] for j in range(half)])

        @pl.when(giver)
        def _():
            carry_copy(way).start()
            carry[way] = jnp.zeros((share, LANES), F32)

    def crossed(way, giver):
        @pl.when(giver)
        def _():
            carry_copy(way).wait_send()

        @pl.when(jnp.logical_not(giver))
        def _():
            carry_copy(way).wait_recv()

    def lanes(p):
        return slice(p * LANES, (p + 1) * LANES)

    def pair_of(ref, p):
        return ref[p * slots : (p + 1) * slots].reshape(HEAD_DIM, LANES)

    loads[0].wait()
    loads[1].wait()
    for p in range(pairs):
        packed = pack(tn(k[:, lanes(p)], v[:, lanes(p)]))
        kv[p * slots : (p + 1) * slots] = packed.reshape(slots, share, LANES)
    pl.semaphore_wait(barrier, len(mates) + len(twins))
    scatter(0, kv, kv_in)

    loads[2].wait()
    t = lax.broadcasted_iota(jnp.int32, (2 * GROUP, GROUP), 0) % GROUP
    causal = t >= lax.broadcasted_iota(jnp.int32, (2 * GROUP, GROUP), 1)

    def within(p):
        s = jnp.where(causal, nt(by_head(q[:, lanes(p)]), k[:, lanes(p)]), 0.0).astype(BF16)
        scores[p] = s
        attn[:, lanes(p)] = nn(side_by_side(s), by_head(v[:, lanes(p)]))

    for p in range(pairs // 2):
        within(p)

    landed(0, kv_in)
    cross(0, kv_in, upper == 0)
    for p in range(pairs // 2, 3 * pairs // 4):
        within(p)
    crossed(0, upper == 0)
    total = carry[0]
    for j in range(half):
        prefix[j] = total
        total = total + kv_in[j]
    scatter(1, prefix, state)
    for p in range(3 * pairs // 4, pairs):
        within(p)
    loads[3].wait()
    loads[4].wait()
    landed(1, state)

    squares = jnp.zeros((GROUP, LANES), F32)
    cross_sum = jnp.zeros((GROUP, LANES), F32)
    for p in range(pairs):
        a = attn[:, lanes(p)] + nn(q[:, lanes(p)], unpack(pair_of(state, p)))
        attn[:, lanes(p)] = a
        squares += a * a
        cross_sum += a * (g[:, lanes(p)].astype(F32) * gain_ref[:, lanes(p)])
    inv = lax.rsqrt(jnp.sum(squares, 1, keepdims=True) / width + 1e-06)
    mean = jnp.sum(cross_sum, 1, keepdims=True) * inv / width
    gain_rows = []
    for p in range(pairs):
        normed = attn[:, lanes(p)] * inv
        gf = g[:, lanes(p)].astype(F32)
        ga = (inv * (gf * gain_ref[:, lanes(p)] - normed * mean)).astype(BF16)
        grad_attn[:, lanes(p)] = ga
        packed = pack(tn(q[:, lanes(p)], ga))
        qd[p * slots : (p + 1) * slots, :share] = packed.reshape(slots, share, LANES)
        gain_rows.append(jnp.sum(gf * normed, 0, keepdims=True))
    gain_tile = jnp.concatenate(gain_rows, 0)
    for j in range(half):
        qd[j, share:] = gain_tile
    scatter(2, qd, qd_in)

    def after(p):
        normed = attn[:, lanes(p)] * inv
        o_out[:, lanes(p)] = (normed * gain_ref[:, lanes(p)]).astype(BF16)
        ga = grad_attn[:, lanes(p)]
        ga2 = by_head(ga)
        ds = jnp.where(causal, nt(ga2, v[:, lanes(p)]), 0.0).astype(BF16)
        gq = nn(side_by_side(ds), by_head(k[:, lanes(p)]))
        gq = gq + nt(ga, unpack(pair_of(state, p)))
        gq_out[:, lanes(p)] = gq.astype(BF16)
        gk_part[:, lanes(p)] = tn(ds, by_head(q[:, lanes(p)]))
        gv_part[:, lanes(p)] = tn(scores[p], ga2)

    for p in range(pairs // 2):
        after(p)

    landed(2, qd_in)
    cross(1, qd_in, upper == 1)
    slot = 2 * row + upper
    gains[slot] = functools.reduce(jnp.add, [qd_in[j, share:] for j in range(half)])
    for d, c in twins:
        pltpu.make_async_remote_copy(
            src_ref=gains.at[slot],
            dst_ref=gains.at[slot],
            send_sem=gain_send,
            recv_sem=gain_recv,
            device_id={"dp": d, "ctx": c},
            device_id_type=MESH,
        ).start()
    for p in range(pairs // 2, 3 * pairs // 4):
        after(p)
    crossed(1, upper == 1)
    total = carry[1]
    for j in range(half - 1, -1, -1):
        suffix[j] = total
        total = total + qd_in[j, :share]
    scatter(3, suffix, later)
    for p in range(3 * pairs // 4, pairs):
        after(p)

    rest = gains.at[pl.ds(0, len(twins))]
    pltpu.make_async_copy(rest, rest, gain_recv).wait()
    gg_ref[...] = functools.reduce(jnp.add, [gains[j] for j in range(2 * ndp)])
    pltpu.make_async_copy(rest, rest, gain_send).wait()
    left(0, kv)
    left(1, prefix)
    left(2, qd)
    left(3, suffix)
    landed(3, later)


def last_kernel(
    k, v, o, gq, gk_part, gv_part, later, gg,
    out_hbm, gq_hbm, gk_hbm, gv_hbm, gg_hbm, gk_out, gv_out, sems,
):
    stores = []

    def store(src, dst):
        stores.append(pltpu.make_async_copy(src, dst, sems.at[len(stores)]))
        stores[-1].start()

    store(o, out_hbm.at[0])
    store(gq, gq_hbm.at[0])
    store(gg, gg_hbm)
    width = k.shape[1]
    for p in range(width // LANES):
        lanes = slice(p * LANES, (p + 1) * LANES)
        low = unpack(later[p * HEAD_DIM : (p + 1) * HEAD_DIM])
        gk_out[:, lanes] = (gk_part[:, lanes] + nt(v[:, lanes], low)).astype(BF16)
        gv_out[:, lanes] = (gv_part[:, lanes] + nn(k[:, lanes], low)).astype(BF16)
    store(gk_out, gk_hbm.at[0])
    store(gv_out, gv_hbm.at[0])
    for copy in stores:
        copy.wait()


def pinned(x):
    return pltpu.with_memory_space_constraint(x, pltpu.HBM)


def per_device(n, ndp, queries, keys, values, gain, grad_out):
    rows, width = queries.shape[1:]
    pairs = width // LANES
    half = n // 2
    share = pairs * HEAD_DIM // half
    gain_rows = width // LANES
    flat = jax.ShapeDtypeStruct((1, rows, width), BF16)
    low_out = jax.ShapeDtypeStruct((rows, width), BF16)
    full_out = jax.ShapeDtypeStruct((rows, width), F32)
    gain_out = jax.ShapeDtypeStruct((gain_rows, LANES), F32)
    hbm = pl.BlockSpec(memory_space=pltpu.HBM)
    vmem = pl.BlockSpec(memory_space=pltpu.VMEM)
    low = pltpu.VMEM((rows, width), BF16)
    full = pltpu.VMEM((rows, width), F32)
    part = pltpu.VMEM((half, share, LANES), F32)
    wide = pltpu.VMEM((half, share + gain_rows, LANES), F32)
    pair = pltpu.VMEM((2, share, LANES), F32)
    dma = pltpu.SemaphoreType.DMA
    k, v, o, gq, gk, gv, later, gg = pl.pallas_call(
        functools.partial(scan_kernel, n, ndp),
        out_shape=[low_out] * 4
        + [full_out] * 2
        + [jax.ShapeDtypeStruct((half, share, LANES), F32), gain_out],
        in_specs=[hbm] * 5,
        out_specs=[vmem] * 8,
        scratch_shapes=[low, low, pltpu.VMEM((1, width), F32), full, low]
        + [pltpu.VMEM((pairs, 2 * GROUP, GROUP), BF16)]
        + [part] * 4
        + [wide, wide, part, pair, pair, pltpu.VMEM((2 * ndp, gain_rows, LANES), F32)]
        + [dma((5,)), dma((4,)), dma((4,)), dma((2,)), dma((2,)), dma, dma],
        compiler_params=pltpu.CompilerParams(
            collective_id=0, has_side_effects=True, vmem_limit_bytes=32 * 2**20
        ),
        name="linear_attention",
    )(*(pinned(x) for x in (queries, keys, values, gain.reshape(1, width), grad_out)))
    out, gq, gk, gv, gg = pl.pallas_call(
        last_kernel,
        out_shape=[flat] * 4 + [gain_out],
        in_specs=[vmem] * 8,
        out_specs=[hbm] * 5,
        scratch_shapes=[low, low, dma((5,))],
        compiler_params=pltpu.CompilerParams(vmem_limit_bytes=32 * 2**20),
        name="last_products",
    )(k, v, o, gq, gk, gv, later.reshape(pairs * HEAD_DIM, LANES), gg)
    return out, gq, gk, gv, gg.reshape(width)


def solution(mesh):
    spec = P("dp", "ctx", None)
    return jax.shard_map(
        functools.partial(per_device, mesh.shape["ctx"], mesh.shape["dp"]),
        mesh=mesh,
        in_specs=(spec, spec, spec, P(), spec),
        out_specs=(spec, spec, spec, spec, P()),
        check_vma=False,
    )
```

```python
import functools

import jax
import jax.numpy as jnp
from jax import lax
from jax.experimental import pallas as pl
from jax.experimental.pallas import tpu as pltpu
from jax.sharding import PartitionSpec as P

HEAD_DIM = 64
GROUP = 128
LANES = 2 * HEAD_DIM
F32 = jnp.float32
BF16 = jnp.bfloat16
MESH = pl.DeviceIdType.MESH


def nn(a, b):
    return lax.dot_general(a, b, (((1,), (0,)), ((), ())), preferred_element_type=F32)


def nt(a, b):
    return lax.dot_general(a, b, (((1,), (1,)), ((), ())), preferred_element_type=F32)


def tn(a, b):
    return lax.dot_general(a, b, (((0,), (0,)), ((), ())), preferred_element_type=F32)


def first_head(rows):
    return lax.broadcasted_iota(jnp.int32, (rows, LANES), 1) < HEAD_DIM


def by_head(x):
    mask = first_head(x.shape[0])
    zero = jnp.zeros_like(x)
    return jnp.concatenate([jnp.where(mask, x, zero), jnp.where(mask, zero, x)], 0)


def pack(square):
    mask = first_head(HEAD_DIM)
    return jnp.where(mask, square[:HEAD_DIM], square[HEAD_DIM:])


def unpack(packed):
    mask = first_head(HEAD_DIM)
    zero = jnp.zeros_like(packed)
    both = [jnp.where(mask, packed, zero), jnp.where(mask, zero, packed)]
    return jnp.concatenate(both, 0).astype(BF16)


def side_by_side(stacked):
    return jnp.concatenate([stacked[:GROUP], stacked[GROUP:]], 1)


def scan_kernel(
    n, ndp, q_hbm, k_hbm, v_hbm, gain_hbm, g_hbm,
    k, v, o_out, gq_out, gk_part, gv_part, later,
    q, g, gain_ref, attn, grad_attn, scores,
    kv, kv_in, prefix, state, qd, qd_in, suffix, sums, carry, gains,
    in_sems, send_sems, recv_sems, carry_send, carry_recv, gain_send, gain_recv,
):
    me = lax.axis_index("ctx")
    row = lax.axis_index("dp")
    width = q.shape[1]
    pairs = width // LANES
    share = kv.shape[1]
    slots = HEAD_DIM // share
    half = n // 2
    upper = me // half
    place = lax.rem(me, half)
    other = lax.rem(me + half, n)
    cut = share // 2
    rows_of = ((0, cut), (cut, share - cut))

    barrier = pltpu.get_barrier_semaphore()
    loads = []
    arrays = (k_hbm.at[0], k), (v_hbm.at[0], v), (q_hbm.at[0], q), (g_hbm.at[0], g)
    for i, (src, dst) in enumerate(arrays + ((gain_hbm, gain_ref),)):
        loads.append(pltpu.make_async_copy(src, dst, in_sems.at[i]))
        loads[-1].start()

    mates = [lax.rem(place + hop, half) for hop in range(1, half)]
    twins = [(lax.rem(row + d, ndp), c) for d in range(ndp) for c in (me, other)][1:]
    for mate in mates:
        pl.semaphore_signal(
            barrier, inc=1, device_id={"ctx": upper * half + mate}, device_id_type=MESH
        )
    for d, c in twins:
        pl.semaphore_signal(barrier, inc=1, device_id={"dp": d, "ctx": c}, device_id_type=MESH)

    turns = []
    for i in range(pairs):
        pair = lax.rem(place // slots + 1 + i, pairs)
        owners = [pair * slots + lax.rem(place + h, slots) for h in range(slots)]
        turns.append((pair, owners[1:] if i == pairs - 1 else owners))

    def chunk(ref, index, c, extra):
        start, size = rows_of[c]
        return ref.at[index, pl.ds(start, size + (extra if c else 0))]

    def send(phase, c, source, target, mate, extra=0):
        pltpu.make_async_remote_copy(
            src_ref=chunk(source, mate, c, extra),
            dst_ref=chunk(target, place, c, extra),
            send_sem=send_sems.at[phase, c],
            recv_sem=recv_sems.at[phase, c],
            device_id={"ctx": upper * half + mate},
            device_id_type=MESH,
        ).start()

    def landed(phase, c, target, extra=0):
        rest = chunk(target, pl.ds(0, half - 1), c, extra)
        pltpu.make_async_copy(rest, rest, recv_sems.at[phase, c]).wait()

    def left(phase, source, extra=0):
        for c in range(2):
            rest = chunk(source, pl.ds(0, half - 1), c, extra)
            pltpu.make_async_copy(rest, rest, send_sems.at[phase, c]).wait()

    def carry_copy(way, c):
        here = pl.ds(*rows_of[c])
        return pltpu.make_async_remote_copy(
            src_ref=sums.at[way, here],
            dst_ref=carry.at[way, here],
            send_sem=carry_send.at[way, c],
            recv_sem=carry_recv.at[way, c],
            device_id={"ctx": other},
            device_id_type=MESH,
        )

    def cross(way, c, arrived, giver):
        start, size = rows_of[c]
        here = slice(start, start + size)
        sums[way, here] = functools.reduce(jnp.add, [arrived[j, here] for j in range(half)])

        @pl.when(giver)
        def _():
            carry_copy(way, c).start()
            carry[way, here] = jnp.zeros((size, LANES), F32)

    def crossed(way, c, giver):
        @pl.when(giver)
        def _():
            carry_copy(way, c).wait_send()

        @pl.when(jnp.logical_not(giver))
        def _():
            carry_copy(way, c).wait_recv()

    def scan(way, c, arrived, result, order):
        start, size = rows_of[c]
        here = slice(start, start + size)
        total = carry[way, here]
        for j in order:
            result[j, here] = total
            total = total + arrived[j, here]

    def lanes(p):
        if isinstance(p, int):
            return slice(p * LANES, (p + 1) * LANES)
        return pl.ds(pl.multiple_of(p * LANES, LANES), LANES)

    def pair_of(ref, p):
        return ref[p * slots : (p + 1) * slots].reshape(HEAD_DIM, LANES)

    def put(ref, pair, packed):
        ref[pl.ds(pair * slots, slots), :share] = packed.reshape(slots, share, LANES)

    loads[0].wait()
    loads[1].wait()
    for i, (pair, owners) in enumerate(turns):
        put(kv, pair, pack(tn(k[:, lanes(pair)], v[:, lanes(pair)])))
        if i == 0:
            pl.semaphore_wait(barrier, len(mates) + len(twins))
        for owner in owners:
            send(0, 0, kv, kv_in, owner)
    for pair, owners in turns:
        for owner in owners:
            send(0, 1, kv, kv_in, owner)
    kv_in[place] = kv[place]

    loads[2].wait()
    t = lax.broadcasted_iota(jnp.int32, (2 * GROUP, GROUP), 0) % GROUP
    causal = t >= lax.broadcasted_iota(jnp.int32, (2 * GROUP, GROUP), 1)

    def within(first, last):
        for p in range(pairs * first // 8, pairs * last // 8):
            s = nt(by_head(q[:, lanes(p)]), k[:, lanes(p)])
            s = jnp.where(causal, s, 0.0).astype(BF16)
            scores[p] = s
            attn[:, lanes(p)] = nn(side_by_side(s), by_head(v[:, lanes(p)]))

    ahead = range(half)
    lower = upper == 0
    within(0, 4)
    landed(0, 0, kv_in)
    cross(0, 0, kv_in, lower)
    within(4, 6)
    landed(0, 1, kv_in)
    cross(0, 1, kv_in, lower)
    crossed(0, 0, lower)
    scan(0, 0, kv_in, prefix, ahead)
    for mate in mates:
        send(1, 0, prefix, state, mate)
    crossed(0, 1, lower)
    scan(0, 1, kv_in, prefix, ahead)
    for mate in mates:
        send(1, 1, prefix, state, mate)
    state[place] = prefix[place]
    within(6, 8)
    loads[3].wait()
    loads[4].wait()
    landed(1, 0, state)
    landed(1, 1, state)

    squares = jnp.zeros((GROUP, LANES), F32)
    cross_sum = jnp.zeros((GROUP, LANES), F32)
    for p in range(pairs):
        a = attn[:, lanes(p)] + nn(q[:, lanes(p)], unpack(pair_of(state, p)))
        attn[:, lanes(p)] = a
        squares += a * a
        cross_sum += a * (g[:, lanes(p)].astype(F32) * gain_ref[:, lanes(p)])
    inv = lax.rsqrt(jnp.sum(squares, 1, keepdims=True) / width + 1e-06)
    mean = jnp.sum(cross_sum, 1, keepdims=True) * inv / width
    tile = qd.shape[1] - share
    for pair, owners in turns:
        normed = attn[:, lanes(pair)] * inv
        gf = g[:, lanes(pair)].astype(F32)
        ga = (inv * (gf * gain_ref[:, lanes(pair)] - normed * mean)).astype(BF16)
        grad_attn[:, lanes(pair)] = ga
        put(qd, pair, pack(tn(q[:, lanes(pair)], ga)))
        gain_tile = jnp.sum((gf * normed).reshape(GROUP // tile, tile, LANES), 0)
        for h in range(slots):
            qd[pair * slots + h, share:] = gain_tile
        for owner in owners:
            send(2, 0, qd, qd_in, owner)
    for pair, owners in turns:
        for owner in owners:
            send(2, 1, qd, qd_in, owner, tile)
    qd_in[place] = qd[place]

    def after(first, last):
        for p in range(pairs * first // 8, pairs * last // 8):
            normed = attn[:, lanes(p)] * inv
            o_out[:, lanes(p)] = (normed * gain_ref[:, lanes(p)]).astype(BF16)
            ga = grad_attn[:, lanes(p)]
            ga2 = by_head(ga)
            ds = jnp.where(causal, nt(ga2, v[:, lanes(p)]), 0.0).astype(BF16)
            gq = nn(side_by_side(ds), by_head(k[:, lanes(p)]))
            gq = gq + nt(ga, unpack(pair_of(state, p)))
            gq_out[:, lanes(p)] = gq.astype(BF16)
            gk_part[:, lanes(p)] = tn(ds, by_head(q[:, lanes(p)]))
            gv_part[:, lanes(p)] = tn(scores[p], ga2)

    back = range(half - 1, -1, -1)
    raised = upper == 1
    after(0, 3)
    landed(2, 0, qd_in)
    cross(1, 0, qd_in, raised)
    after(3, 4)
    landed(2, 1, qd_in, tile)
    cross(1, 1, qd_in, raised)
    slot = 2 * row + upper
    gains[slot] = functools.reduce(jnp.add, [qd_in[j, share:] for j in range(half)])
    for d, c in twins:
        pltpu.make_async_remote_copy(
            src_ref=gains.at[slot],
            dst_ref=gains.at[slot],
            send_sem=gain_send,
            recv_sem=gain_recv,
            device_id={"dp": d, "ctx": c},
            device_id_type=MESH,
        ).start()
    after(4, 5)
    crossed(1, 0, raised)
    scan(1, 0, qd_in, suffix, back)
    for mate in mates:
        send(3, 0, suffix, later, mate)
    crossed(1, 1, raised)
    scan(1, 1, qd_in, suffix, back)
    rest = gains.at[pl.ds(0, len(twins))]
    pltpu.make_async_copy(rest, rest, gain_recv).wait()
    gain_sum = functools.reduce(jnp.add, [gains[j] for j in range(2 * ndp)])
    for j in range(half):
        suffix[j, share:] = gain_sum
    for mate in mates:
        send(3, 1, suffix, later, mate, tile)
    later[place] = suffix[place]
    after(5, 8)

    pltpu.make_async_copy(rest, rest, gain_send).wait()
    left(0, kv)
    left(1, prefix)
    left(2, qd, tile)
    left(3, suffix, tile)
    landed(3, 0, later)
    landed(3, 1, later, tile)


def last_kernel(
    share, k, v, o, gq, gk_part, gv_part, later,
    out_hbm, gq_hbm, gk_hbm, gv_hbm, gg_hbm, gk_out, gv_out, gg, sems,
):
    stores = []

    def store(src, dst):
        stores.append(pltpu.make_async_copy(src, dst, sems.at[len(stores)]))
        stores[-1].start()

    store(o, out_hbm.at[0])
    store(gq, gq_hbm.at[0])
    width = k.shape[1]
    slots = HEAD_DIM // share
    for p in range(width // LANES):
        gg[p : p + 1] = jnp.sum(later[p * slots, share:], 0, keepdims=True)
    store(gg, gg_hbm)
    for p in range(width // LANES):
        lanes = slice(p * LANES, (p + 1) * LANES)
        low = later[p * slots : (p + 1) * slots, :share].reshape(HEAD_DIM, LANES)
        low = unpack(low)
        gk_out[:, lanes] = (gk_part[:, lanes] + nt(v[:, lanes], low)).astype(BF16)
        gv_out[:, lanes] = (gv_part[:, lanes] + nn(k[:, lanes], low)).astype(BF16)
    store(gk_out, gk_hbm.at[0])
    store(gv_out, gv_hbm.at[0])
    for copy in stores:
        copy.wait()


def pinned(x):
    return pltpu.with_memory_space_constraint(x, pltpu.HBM)


def per_device(n, ndp, queries, keys, values, gain, grad_out):
    rows, width = queries.shape[1:]
    pairs = width // LANES
    half = n // 2
    share = pairs * HEAD_DIM // half
    gain_rows = width // LANES
    flat = jax.ShapeDtypeStruct((1, rows, width), BF16)
    low_out = jax.ShapeDtypeStruct((rows, width), BF16)
    full_out = jax.ShapeDtypeStruct((rows, width), F32)
    gain_out = jax.ShapeDtypeStruct((gain_rows, LANES), F32)
    hbm = pl.BlockSpec(memory_space=pltpu.HBM)
    vmem = pl.BlockSpec(memory_space=pltpu.VMEM)
    low = pltpu.VMEM((rows, width), BF16)
    full = pltpu.VMEM((rows, width), F32)
    part = pltpu.VMEM((half, share, LANES), F32)
    tile = 8
    wide = pltpu.VMEM((half, share + tile, LANES), F32)
    pair = pltpu.VMEM((2, share, LANES), F32)
    dma = pltpu.SemaphoreType.DMA
    k, v, o, gq, gk, gv, later = pl.pallas_call(
        functools.partial(scan_kernel, n, ndp),
        out_shape=[low_out] * 4
        + [full_out] * 2
        + [jax.ShapeDtypeStruct((half, share + tile, LANES), F32)],
        in_specs=[hbm] * 5,
        out_specs=[vmem] * 7,
        scratch_shapes=[low, low, pltpu.VMEM((1, width), F32), full, low]
        + [pltpu.VMEM((pairs, 2 * GROUP, GROUP), BF16)]
        + [part] * 4
        + [wide] * 3
        + [pair, pair, pltpu.VMEM((2 * ndp, tile, LANES), F32)]
        + [dma((5,)), dma((4, 2)), dma((4, 2)), dma((2, 2)), dma((2, 2)), dma, dma],
        compiler_params=pltpu.CompilerParams(
            collective_id=0, has_side_effects=True, vmem_limit_bytes=32 * 2**20
        ),
        name="linear_attention",
    )(*(pinned(x) for x in (queries, keys, values, gain.reshape(1, width), grad_out)))
    out, gq, gk, gv, gg = pl.pallas_call(
        functools.partial(last_kernel, share),
        out_shape=[flat] * 4 + [gain_out],
        in_specs=[vmem] * 7,
        out_specs=[hbm] * 5,
        scratch_shapes=[low, low, pltpu.VMEM((gain_rows, LANES), F32), dma((5,))],
        compiler_params=pltpu.CompilerParams(vmem_limit_bytes=32 * 2**20),
        name="last_products",
    )(k, v, o, gq, gk, gv, later)
    return out, gq, gk, gv, gg.reshape(width)


def solution(mesh):
    spec = P("dp", "ctx", None)
    return jax.shard_map(
        functools.partial(per_device, mesh.shape["ctx"], mesh.shape["dp"]),
        mesh=mesh,
        in_specs=(spec, spec, spec, P(), spec),
        out_specs=(spec, spec, spec, spec, P()),
        check_vma=False,
    )
```

```python
import functools

import jax
import jax.numpy as jnp
from jax import lax
from jax.experimental import pallas as pl
from jax.experimental.pallas import tpu as pltpu
from jax.sharding import PartitionSpec as P

HEAD_DIM = 64
GROUP = 128
LANES = 2 * HEAD_DIM
F32 = jnp.float32
BF16 = jnp.bfloat16
MESH = pl.DeviceIdType.MESH


def nn(a, b):
    return lax.dot_general(a, b, (((1,), (0,)), ((), ())), preferred_element_type=F32)


def nt(a, b):
    return lax.dot_general(a, b, (((1,), (1,)), ((), ())), preferred_element_type=F32)


def tn(a, b):
    return lax.dot_general(a, b, (((0,), (0,)), ((), ())), preferred_element_type=F32)


def first_head(rows):
    return lax.broadcasted_iota(jnp.int32, (rows, LANES), 1) < HEAD_DIM


def by_head(x):
    mask = first_head(x.shape[0])
    zero = jnp.zeros_like(x)
    return jnp.concatenate([jnp.where(mask, x, zero), jnp.where(mask, zero, x)], 0)


def pack(square):
    mask = first_head(HEAD_DIM)
    return jnp.where(mask, square[:HEAD_DIM], square[HEAD_DIM:])


def unpack(packed):
    mask = first_head(HEAD_DIM)
    zero = jnp.zeros_like(packed)
    both = [jnp.where(mask, packed, zero), jnp.where(mask, zero, packed)]
    return jnp.concatenate(both, 0).astype(BF16)


def side_by_side(stacked):
    return jnp.concatenate([stacked[:GROUP], stacked[GROUP:]], 1)


def scan_kernel(
    n, ndp, q_hbm, k_hbm, v_hbm, gain_hbm, g_hbm,
    k, v, o_out, gq_out, gk_part, gv_part, later,
    q, g, gain_ref, attn, grad_attn, scores, q_turned,
    kv, kv_in, prefix, state, qd, qd_in, suffix, sums, carry, gains,
    in_sems, send_sems, recv_sems, carry_send, carry_recv, gain_send, gain_recv,
):
    me = lax.axis_index("ctx")
    row = lax.axis_index("dp")
    width = q.shape[1]
    pairs = width // LANES
    group = pairs // 2
    share = kv.shape[2]
    slots = HEAD_DIM // share
    half = n // 2
    upper = me // half
    place = lax.rem(me, half)
    other = lax.rem(me + half, n)

    barrier = pltpu.get_barrier_semaphore()
    loads = []
    arrays = (k_hbm.at[0], k), (v_hbm.at[0], v), (q_hbm.at[0], q), (g_hbm.at[0], g)
    for i, (src, dst) in enumerate(arrays + ((gain_hbm, gain_ref),)):
        loads.append(pltpu.make_async_copy(src, dst, in_sems.at[i]))
        loads[-1].start()

    mates = [lax.rem(place + hop, half) for hop in range(1, half)]
    twins = [(lax.rem(row + d, ndp), c) for d in range(ndp) for c in (me, other)][1:]
    for mate in mates:
        pl.semaphore_signal(
            barrier, inc=1, device_id={"ctx": upper * half + mate}, device_id_type=MESH
        )
    for d, c in twins:
        pl.semaphore_signal(barrier, inc=1, device_id={"dp": d, "ctx": c}, device_id_type=MESH)

    def chunk(ref, c, index, extra):
        return ref.at[c, index, pl.ds(0, share + (extra if c else 0))]

    def send(phase, c, source, target, extra=0):
        for mate in mates:
            pltpu.make_async_remote_copy(
                src_ref=chunk(source, c, mate, extra),
                dst_ref=chunk(target, c, place, extra),
                send_sem=send_sems.at[phase, c],
                recv_sem=recv_sems.at[phase, c],
                device_id={"ctx": upper * half + mate},
                device_id_type=MESH,
            ).start()
        target[c, place] = source[c, place]

    def landed(phase, c, target, extra=0):
        rest = chunk(target, c, pl.ds(0, half - 1), extra)
        pltpu.make_async_copy(rest, rest, recv_sems.at[phase, c]).wait()

    def left(phase, source, extra=0):
        for c in range(2):
            rest = chunk(source, c, pl.ds(0, half - 1), extra)
            pltpu.make_async_copy(rest, rest, send_sems.at[phase, c]).wait()

    def carry_copy(way, c):
        return pltpu.make_async_remote_copy(
            src_ref=sums.at[way, c],
            dst_ref=carry.at[way, c],
            send_sem=carry_send.at[way, c],
            recv_sem=carry_recv.at[way, c],
            device_id={"ctx": other},
            device_id_type=MESH,
        )

    def cross(way, c, arrived, giver):
        parts = [arrived[c, j, :share] for j in range(half)]
        sums[way, c] = functools.reduce(jnp.add, parts)

        @pl.when(giver)
        def _():
            carry_copy(way, c).start()
            carry[way, c] = jnp.zeros((share, LANES), F32)

    def crossed(way, c, giver):
        @pl.when(giver)
        def _():
            carry_copy(way, c).wait_send()

        @pl.when(jnp.logical_not(giver))
        def _():
            carry_copy(way, c).wait_recv()

    def scan(way, c, arrived, result, order):
        total = carry[way, c]
        for j in order:
            result[c, j, :share] = total
            total = total + arrived[c, j, :share]

    def lanes(p):
        return slice(p * LANES, (p + 1) * LANES)

    def place_of(p):
        return p // group, p % group * HEAD_DIM // share

    def pair_of(ref, p):
        c, first = place_of(p)
        return ref[c, first : first + slots, :share].reshape(HEAD_DIM, LANES)

    def put(ref, p, packed):
        c, first = place_of(p)
        ref[c, first : first + slots, :share] = packed.reshape(slots, share, LANES)

    loads[0].wait()
    loads[1].wait()
    for c in range(2):
        for p in range(c * group, (c + 1) * group):
            put(kv, p, pack(tn(k[:, lanes(p)], v[:, lanes(p)])))
        if c == 0:
            pl.semaphore_wait(barrier, len(mates) + len(twins))
        send(0, c, kv, kv_in)

    loads[2].wait()
    t = lax.broadcasted_iota(jnp.int32, (2 * GROUP, GROUP), 0) % GROUP
    causal = t >= lax.broadcasted_iota(jnp.int32, (2 * GROUP, GROUP), 1)

    def within(first, last):
        for p in range(pairs * first // 8, pairs * last // 8):
            s = nt(by_head(q[:, lanes(p)]), k[:, lanes(p)])
            s = jnp.where(causal, s, 0.0).astype(BF16)
            scores[p] = s
            q_turned[p] = q[:, lanes(p)].T
            attn[:, lanes(p)] = nn(side_by_side(s), by_head(v[:, lanes(p)]))

    ahead = range(half)
    lower = upper == 0
    within(0, 4)
    landed(0, 0, kv_in)
    cross(0, 0, kv_in, lower)
    within(4, 6)
    landed(0, 1, kv_in)
    cross(0, 1, kv_in, lower)
    crossed(0, 0, lower)
    scan(0, 0, kv_in, prefix, ahead)
    send(1, 0, prefix, state)
    crossed(0, 1, lower)
    scan(0, 1, kv_in, prefix, ahead)
    send(1, 1, prefix, state)
    within(6, 8)
    loads[3].wait()
    loads[4].wait()

    squares = jnp.zeros((GROUP, LANES), F32)
    cross_sum = jnp.zeros((GROUP, LANES), F32)
    for c in range(2):
        landed(1, c, state)
        for p in range(c * group, (c + 1) * group):
            a = attn[:, lanes(p)] + nn(q[:, lanes(p)], unpack(pair_of(state, p)))
            attn[:, lanes(p)] = a
            squares += a * a
            cross_sum += a * (g[:, lanes(p)].astype(F32) * gain_ref[:, lanes(p)])
    inv = lax.rsqrt(jnp.sum(squares, 1, keepdims=True) / width + 1e-06)
    mean = jnp.sum(cross_sum, 1, keepdims=True) * inv / width
    tile = qd.shape[2] - share
    for c in range(2):
        for p in range(c * group, (c + 1) * group):
            normed = attn[:, lanes(p)] * inv
            gf = g[:, lanes(p)].astype(F32)
            ga = (inv * (gf * gain_ref[:, lanes(p)] - normed * mean)).astype(BF16)
            grad_attn[:, lanes(p)] = ga
            put(qd, p, pack(nn(q_turned[p], ga)))
            gain_tile = jnp.sum((gf * normed).reshape(GROUP // tile, tile, LANES), 0)
            for j in range(p * half // pairs, (p + 1) * half // pairs):
                qd[1, j, share:] = gain_tile
        send(2, c, qd, qd_in, tile)

    def after(first, last):
        for p in range(pairs * first // 8, pairs * last // 8):
            normed = attn[:, lanes(p)] * inv
            o_out[:, lanes(p)] = (normed * gain_ref[:, lanes(p)]).astype(BF16)
            ga = grad_attn[:, lanes(p)]
            ga2 = by_head(ga)
            ds = jnp.where(causal, nt(ga2, v[:, lanes(p)]), 0.0).astype(BF16)
            gq = nn(side_by_side(ds), by_head(k[:, lanes(p)]))
            gq = gq + nt(ga, unpack(pair_of(state, p)))
            gq_out[:, lanes(p)] = gq.astype(BF16)
            gk_part[:, lanes(p)] = tn(ds, by_head(q[:, lanes(p)]))
            gv_part[:, lanes(p)] = tn(scores[p], ga2)

    back = range(half - 1, -1, -1)
    raised = upper == 1
    after(0, 3)
    landed(2, 0, qd_in)
    cross(1, 0, qd_in, raised)
    after(3, 4)
    landed(2, 1, qd_in, tile)
    cross(1, 1, qd_in, raised)
    slot = 2 * row + upper
    gains[slot] = functools.reduce(jnp.add, [qd_in[1, j, share:] for j in range(half)])
    for d, c in twins:
        pltpu.make_async_remote_copy(
            src_ref=gains.at[slot],
            dst_ref=gains.at[slot],
            send_sem=gain_send,
            recv_sem=gain_recv,
            device_id={"dp": d, "ctx": c},
            device_id_type=MESH,
        ).start()
    after(4, 5)
    crossed(1, 0, raised)
    scan(1, 0, qd_in, suffix, back)
    send(3, 0, suffix, later, tile)
    crossed(1, 1, raised)
    scan(1, 1, qd_in, suffix, back)
    rest = gains.at[pl.ds(0, len(twins))]
    pltpu.make_async_copy(rest, rest, gain_recv).wait()
    gain_sum = functools.reduce(jnp.add, [gains[j] for j in range(2 * ndp)])
    for j in range(half):
        suffix[1, j, share:] = gain_sum
    send(3, 1, suffix, later, tile)
    after(5, 8)

    pltpu.make_async_copy(rest, rest, gain_send).wait()
    left(0, kv)
    left(1, prefix)
    left(2, qd, tile)
    left(3, suffix, tile)
    landed(3, 0, later)
    landed(3, 1, later, tile)


def last_kernel(
    k, v, o, gq, gk_part, gv_part, later,
    out_hbm, gq_hbm, gk_hbm, gv_hbm, gg_hbm, gk_out, gv_out, gg, sems,
):
    stores = []

    def store(src, dst):
        stores.append(pltpu.make_async_copy(src, dst, sems.at[len(stores)]))
        stores[-1].start()

    store(o, out_hbm.at[0])
    store(gq, gq_hbm.at[0])
    width = k.shape[1]
    pairs = width // LANES
    group = pairs // 2
    half = later.shape[1]
    share = group * HEAD_DIM // half
    for p in range(pairs):
        gg[p : p + 1] = jnp.sum(later[1, p * half // pairs, share:], 0, keepdims=True)
    store(gg, gg_hbm)
    for p in range(pairs):
        lanes = slice(p * LANES, (p + 1) * LANES)
        first = p % group * HEAD_DIM // share
        low = later[p // group, first : first + HEAD_DIM // share, :share]
        low = unpack(low.reshape(HEAD_DIM, LANES))
        gk_out[:, lanes] = (gk_part[:, lanes] + nt(v[:, lanes], low)).astype(BF16)
        gv_out[:, lanes] = (gv_part[:, lanes] + nn(k[:, lanes], low)).astype(BF16)
    store(gk_out, gk_hbm.at[0])
    store(gv_out, gv_hbm.at[0])
    for copy in stores:
        copy.wait()


def pinned(x):
    return pltpu.with_memory_space_constraint(x, pltpu.HBM)


def per_device(n, ndp, queries, keys, values, gain, grad_out):
    rows, width = queries.shape[1:]
    pairs = width // LANES
    half = n // 2
    share = pairs // 2 * HEAD_DIM // half
    gain_rows = width // LANES
    flat = jax.ShapeDtypeStruct((1, rows, width), BF16)
    low_out = jax.ShapeDtypeStruct((rows, width), BF16)
    full_out = jax.ShapeDtypeStruct((rows, width), F32)
    gain_out = jax.ShapeDtypeStruct((gain_rows, LANES), F32)
    hbm = pl.BlockSpec(memory_space=pltpu.HBM)
    vmem = pl.BlockSpec(memory_space=pltpu.VMEM)
    low = pltpu.VMEM((rows, width), BF16)
    full = pltpu.VMEM((rows, width), F32)
    part = pltpu.VMEM((2, half, share, LANES), F32)
    tile = 8
    wide = pltpu.VMEM((2, half, share + tile, LANES), F32)
    pair = pltpu.VMEM((2, 2, share, LANES), F32)
    dma = pltpu.SemaphoreType.DMA
    k, v, o, gq, gk, gv, later = pl.pallas_call(
        functools.partial(scan_kernel, n, ndp),
        out_shape=[low_out] * 4
        + [full_out] * 2
        + [jax.ShapeDtypeStruct((2, half, share + tile, LANES), F32)],
        in_specs=[hbm] * 5,
        out_specs=[vmem] * 7,
        scratch_shapes=[low, low, pltpu.VMEM((1, width), F32), full, low]
        + [pltpu.VMEM((pairs, 2 * GROUP, GROUP), BF16), pltpu.VMEM((pairs, LANES, GROUP), BF16)]
        + [part] * 4
        + [wide] * 3
        + [pair, pair, pltpu.VMEM((2 * ndp, tile, LANES), F32)]
        + [dma((5,)), dma((4, 2)), dma((4, 2)), dma((2, 2)), dma((2, 2)), dma, dma],
        compiler_params=pltpu.CompilerParams(
            collective_id=0, has_side_effects=True, vmem_limit_bytes=32 * 2**20
        ),
        name="linear_attention",
    )(*(pinned(x) for x in (queries, keys, values, gain.reshape(1, width), grad_out)))
    out, gq, gk, gv, gg = pl.pallas_call(
        last_kernel,
        out_shape=[flat] * 4 + [gain_out],
        in_specs=[vmem] * 7,
        out_specs=[hbm] * 5,
        scratch_shapes=[low, low, pltpu.VMEM((gain_rows, LANES), F32), dma((5,))],
        compiler_params=pltpu.CompilerParams(vmem_limit_bytes=32 * 2**20),
        name="last_products",
    )(k, v, o, gq, gk, gv, later)
    return out, gq, gk, gv, gg.reshape(width)


def solution(mesh):
    spec = P("dp", "ctx", None)
    return jax.shard_map(
        functools.partial(per_device, mesh.shape["ctx"], mesh.shape["dp"]),
        mesh=mesh,
        in_specs=(spec, spec, spec, P(), spec),
        out_specs=(spec, spec, spec, spec, P()),
        check_vma=False,
    )
```

```python
import functools

import jax
import jax.numpy as jnp
from jax import lax
from jax.experimental import pallas as pl
from jax.experimental.pallas import tpu as pltpu
from jax.sharding import PartitionSpec as P

HEAD_DIM = 64
GROUP = 128
LANES = 2 * HEAD_DIM
F32 = jnp.float32
BF16 = jnp.bfloat16
MESH = pl.DeviceIdType.MESH


def nn(a, b):
    return lax.dot_general(a, b, (((1,), (0,)), ((), ())), preferred_element_type=F32)


def nt(a, b):
    return lax.dot_general(a, b, (((1,), (1,)), ((), ())), preferred_element_type=F32)


def tn(a, b):
    return lax.dot_general(a, b, (((0,), (0,)), ((), ())), preferred_element_type=F32)


def first_head(rows):
    return lax.broadcasted_iota(jnp.int32, (rows, LANES), 1) < HEAD_DIM


def by_head(x):
    mask = first_head(x.shape[0])
    zero = jnp.zeros_like(x)
    return jnp.concatenate([jnp.where(mask, x, zero), jnp.where(mask, zero, x)], 0)


def pack(square):
    mask = first_head(HEAD_DIM)
    return jnp.where(mask, square[:HEAD_DIM], square[HEAD_DIM:])


def unpack(packed):
    mask = first_head(HEAD_DIM)
    zero = jnp.zeros_like(packed)
    both = [jnp.where(mask, packed, zero), jnp.where(mask, zero, packed)]
    return jnp.concatenate(both, 0).astype(BF16)


def side_by_side(stacked):
    return jnp.concatenate([stacked[:GROUP], stacked[GROUP:]], 1)


def flips(count):
    return sorted(range(1, count), key=lambda mask: (-(mask // 2).bit_count(), mask % 2, mask))


def flipped(place, mask, count):
    out = 0
    bit = 1
    while bit < count:
        out = out + lax.rem(place // bit + (1 if mask & bit else 0), 2) * bit
        bit *= 2
    return out


def scan_kernel(
    n, ndp, q_hbm, k_hbm, v_hbm, gain_hbm, g_hbm,
    k, v, o_out, gq_out, gk_part, gv_part, later,
    q, g, gain_ref, attn, grad_attn, scores, q_turned,
    kv, kv_in, prefix, state, qd, qd_in, suffix, sums, carry, gains,
    in_sems, send_sems, recv_sems, carry_send, carry_recv, gain_send, gain_recv,
):
    me = lax.axis_index("ctx")
    row = lax.axis_index("dp")
    width = q.shape[1]
    pairs = width // LANES
    chunks = kv.shape[0]
    group = pairs // chunks
    share = kv.shape[2]
    slots = HEAD_DIM // share
    half = n // 2
    upper = me // half
    place = lax.rem(me, half)
    other = lax.rem(me + half, n)

    barrier = pltpu.get_barrier_semaphore()
    loads = []
    arrays = (k_hbm.at[0], k), (v_hbm.at[0], v), (q_hbm.at[0], q), (g_hbm.at[0], g)
    for i, (src, dst) in enumerate(arrays + ((gain_hbm, gain_ref),)):
        loads.append(pltpu.make_async_copy(src, dst, in_sems.at[i]))
        loads[-1].start()

    mates = [flipped(place, mask, half) for mask in flips(half)]
    twins = [(lax.rem(row + d, ndp), c) for d in range(ndp) for c in (me, other)][1:]
    for mate in mates:
        pl.semaphore_signal(
            barrier, inc=1, device_id={"ctx": upper * half + mate}, device_id_type=MESH
        )
    for d, c in twins:
        pl.semaphore_signal(barrier, inc=1, device_id={"dp": d, "ctx": c}, device_id_type=MESH)

    def chunk(ref, c, index, extra):
        return ref.at[c, index, pl.ds(0, share + (extra if c == chunks - 1 else 0))]

    def send(phase, c, source, target, extra=0):
        for mate in mates:
            pltpu.make_async_remote_copy(
                src_ref=chunk(source, c, mate, extra),
                dst_ref=chunk(target, c, place, extra),
                send_sem=send_sems.at[phase, c],
                recv_sem=recv_sems.at[phase, c],
                device_id={"ctx": upper * half + mate},
                device_id_type=MESH,
            ).start()
        target[c, place] = source[c, place]

    def landed(phase, c, target, extra=0):
        rest = chunk(target, c, pl.ds(0, half - 1), extra)
        pltpu.make_async_copy(rest, rest, recv_sems.at[phase, c]).wait()

    def left(phase, source, extra=0):
        for c in range(chunks):
            rest = chunk(source, c, pl.ds(0, half - 1), extra)
            pltpu.make_async_copy(rest, rest, send_sems.at[phase, c]).wait()

    def carry_copy(way, c):
        return pltpu.make_async_remote_copy(
            src_ref=sums.at[way, c],
            dst_ref=carry.at[way, c],
            send_sem=carry_send.at[way, c],
            recv_sem=carry_recv.at[way, c],
            device_id={"ctx": other},
            device_id_type=MESH,
        )

    def cross(way, c, arrived, giver):
        parts = [arrived[c, j, :share] for j in range(half)]
        sums[way, c] = functools.reduce(jnp.add, parts)

        @pl.when(giver)
        def _():
            carry_copy(way, c).start()
            carry[way, c] = jnp.zeros((share, LANES), F32)

    def crossed(way, c, giver):
        @pl.when(giver)
        def _():
            carry_copy(way, c).wait_send()

        @pl.when(jnp.logical_not(giver))
        def _():
            carry_copy(way, c).wait_recv()

    def scan(way, c, arrived, result, order):
        total = carry[way, c]
        for j in order:
            result[c, j, :share] = total
            total = total + arrived[c, j, :share]

    def lanes(p):
        return slice(p * LANES, (p + 1) * LANES)

    def place_of(p):
        return p // group, p % group * HEAD_DIM // share

    def pair_of(ref, p):
        c, first = place_of(p)
        return ref[c, first : first + slots, :share].reshape(HEAD_DIM, LANES)

    def put(ref, p, packed):
        c, first = place_of(p)
        ref[c, first : first + slots, :share] = packed.reshape(slots, share, LANES)

    loads[0].wait()
    loads[1].wait()
    for c in range(chunks):
        for p in range(c * group, (c + 1) * group):
            put(kv, p, pack(tn(k[:, lanes(p)], v[:, lanes(p)])))
        if c == 0:
            pl.semaphore_wait(barrier, len(mates) + len(twins))
        send(0, c, kv, kv_in)

    loads[2].wait()
    t = lax.broadcasted_iota(jnp.int32, (2 * GROUP, GROUP), 0) % GROUP
    causal = t >= lax.broadcasted_iota(jnp.int32, (2 * GROUP, GROUP), 1)

    def within(first, last):
        for p in range(pairs * first // 8, pairs * last // 8):
            s = nt(by_head(q[:, lanes(p)]), k[:, lanes(p)])
            s = jnp.where(causal, s, 0.0).astype(BF16)
            scores[p] = s
            q_turned[p] = q[:, lanes(p)].T
            attn[:, lanes(p)] = nn(side_by_side(s), by_head(v[:, lanes(p)]))

    ahead = range(half)
    lower = upper == 0
    within(0, 3)
    for c in range(chunks):
        landed(0, c, kv_in)
        cross(0, c, kv_in, lower)
        if c < chunks - 1:
            within(3 + c, 4 + c)
    for c in range(chunks):
        crossed(0, c, lower)
        scan(0, c, kv_in, prefix, ahead)
        send(1, c, prefix, state)
    within(2 + chunks, 8)
    loads[3].wait()
    loads[4].wait()

    squares = jnp.zeros((GROUP, LANES), F32)
    cross_sum = jnp.zeros((GROUP, LANES), F32)
    for c in range(chunks):
        landed(1, c, state)
        for p in range(c * group, (c + 1) * group):
            a = attn[:, lanes(p)] + nn(q[:, lanes(p)], unpack(pair_of(state, p)))
            attn[:, lanes(p)] = a
            squares += a * a
            cross_sum += a * (g[:, lanes(p)].astype(F32) * gain_ref[:, lanes(p)])
    inv = lax.rsqrt(jnp.sum(squares, 1, keepdims=True) / width + 1e-06)
    mean = jnp.sum(cross_sum, 1, keepdims=True) * inv / width
    tile = qd.shape[2] - share
    for c in range(chunks):
        for p in range(c * group, (c + 1) * group):
            normed = attn[:, lanes(p)] * inv
            gf = g[:, lanes(p)].astype(F32)
            ga = (inv * (gf * gain_ref[:, lanes(p)] - normed * mean)).astype(BF16)
            grad_attn[:, lanes(p)] = ga
            put(qd, p, pack(nn(q_turned[p], ga)))
            gain_tile = jnp.sum((gf * normed).reshape(GROUP // tile, tile, LANES), 0)
            for j in range(p * half // pairs, (p + 1) * half // pairs):
                qd[chunks - 1, j, share:] = gain_tile
        send(2, c, qd, qd_in, tile)

    def after(first, last):
        for p in range(pairs * first // 8, pairs * last // 8):
            normed = attn[:, lanes(p)] * inv
            o_out[:, lanes(p)] = (normed * gain_ref[:, lanes(p)]).astype(BF16)
            ga = grad_attn[:, lanes(p)]
            ga2 = by_head(ga)
            ds = jnp.where(causal, nt(ga2, v[:, lanes(p)]), 0.0).astype(BF16)
            gq = nn(side_by_side(ds), by_head(k[:, lanes(p)]))
            gq = gq + nt(ga, unpack(pair_of(state, p)))
            gq_out[:, lanes(p)] = gq.astype(BF16)
            gk_part[:, lanes(p)] = tn(ds, by_head(q[:, lanes(p)]))
            gv_part[:, lanes(p)] = tn(scores[p], ga2)

    back = range(half - 1, -1, -1)
    raised = upper == 1
    after(0, 2)
    for c in range(chunks):
        landed(2, c, qd_in, tile)
        cross(1, c, qd_in, raised)
        if c < chunks - 1:
            after(2 + c, 3 + c)
    slot = 2 * row + upper
    gains[slot] = functools.reduce(jnp.add, [qd_in[chunks - 1, j, share:] for j in range(half)])
    for d, c in twins:
        pltpu.make_async_remote_copy(
            src_ref=gains.at[slot],
            dst_ref=gains.at[slot],
            send_sem=gain_send,
            recv_sem=gain_recv,
            device_id={"dp": d, "ctx": c},
            device_id_type=MESH,
        ).start()
    rest = gains.at[pl.ds(0, len(twins))]
    for c in range(chunks):
        crossed(1, c, raised)
        scan(1, c, qd_in, suffix, back)
        if c == chunks - 1:
            pltpu.make_async_copy(rest, rest, gain_recv).wait()
            gain_sum = functools.reduce(jnp.add, [gains[j] for j in range(2 * ndp)])
            for j in range(half):
                suffix[c, j, share:] = gain_sum
        send(3, c, suffix, later, tile)
    after(1 + chunks, 8)

    pltpu.make_async_copy(rest, rest, gain_send).wait()
    left(0, kv)
    left(1, prefix)
    left(2, qd, tile)
    left(3, suffix, tile)
    for c in range(chunks):
        landed(3, c, later, tile)


def last_kernel(
    k, v, o, gq, gk_part, gv_part, later,
    out_hbm, gq_hbm, gk_hbm, gv_hbm, gg_hbm, gk_out, gv_out, gg, sems,
):
    stores = []

    def store(src, dst):
        stores.append(pltpu.make_async_copy(src, dst, sems.at[len(stores)]))
        stores[-1].start()

    store(o, out_hbm.at[0])
    store(gq, gq_hbm.at[0])
    width = k.shape[1]
    pairs = width // LANES
    chunks, half = later.shape[:2]
    group = pairs // chunks
    share = group * HEAD_DIM // half
    for p in range(pairs):
        gg[p : p + 1] = jnp.sum(later[chunks - 1, p * half // pairs, share:], 0, keepdims=True)
    store(gg, gg_hbm)
    for p in range(pairs):
        lanes = slice(p * LANES, (p + 1) * LANES)
        first = p % group * HEAD_DIM // share
        low = later[p // group, first : first + HEAD_DIM // share, :share]
        low = unpack(low.reshape(HEAD_DIM, LANES))
        gk_out[:, lanes] = (gk_part[:, lanes] + nt(v[:, lanes], low)).astype(BF16)
        gv_out[:, lanes] = (gv_part[:, lanes] + nn(k[:, lanes], low)).astype(BF16)
    store(gk_out, gk_hbm.at[0])
    store(gv_out, gv_hbm.at[0])
    for copy in stores:
        copy.wait()


def pinned(x):
    return pltpu.with_memory_space_constraint(x, pltpu.HBM)


def per_device(n, ndp, queries, keys, values, gain, grad_out):
    rows, width = queries.shape[1:]
    pairs = width // LANES
    half = n // 2
    chunks = 4 if pairs * HEAD_DIM // half >= 32 else 2
    share = pairs // chunks * HEAD_DIM // half
    gain_rows = width // LANES
    flat = jax.ShapeDtypeStruct((1, rows, width), BF16)
    low_out = jax.ShapeDtypeStruct((rows, width), BF16)
    full_out = jax.ShapeDtypeStruct((rows, width), F32)
    gain_out = jax.ShapeDtypeStruct((gain_rows, LANES), F32)
    hbm = pl.BlockSpec(memory_space=pltpu.HBM)
    vmem = pl.BlockSpec(memory_space=pltpu.VMEM)
    low = pltpu.VMEM((rows, width), BF16)
    full = pltpu.VMEM((rows, width), F32)
    part = pltpu.VMEM((chunks, half, share, LANES), F32)
    tile = 8
    wide = pltpu.VMEM((chunks, half, share + tile, LANES), F32)
    pair = pltpu.VMEM((2, chunks, share, LANES), F32)
    dma = pltpu.SemaphoreType.DMA
    k, v, o, gq, gk, gv, later = pl.pallas_call(
        functools.partial(scan_kernel, n, ndp),
        out_shape=[low_out] * 4
        + [full_out] * 2
        + [jax.ShapeDtypeStruct((chunks, half, share + tile, LANES), F32)],
        in_specs=[hbm] * 5,
        out_specs=[vmem] * 7,
        scratch_shapes=[low, low, pltpu.VMEM((1, width), F32), full, low]
        + [pltpu.VMEM((pairs, 2 * GROUP, GROUP), BF16), pltpu.VMEM((pairs, LANES, GROUP), BF16)]
        + [part] * 4
        + [wide] * 3
        + [pair, pair, pltpu.VMEM((2 * ndp, tile, LANES), F32)]
        + [dma((5,))] + [dma((4, chunks))] * 2 + [dma((2, chunks))] * 2 + [dma, dma],
        compiler_params=pltpu.CompilerParams(
            collective_id=0, has_side_effects=True, vmem_limit_bytes=32 * 2**20
        ),
        name="linear_attention",
    )(*(pinned(x) for x in (queries, keys, values, gain.reshape(1, width), grad_out)))
    out, gq, gk, gv, gg = pl.pallas_call(
        last_kernel,
        out_shape=[flat] * 4 + [gain_out],
        in_specs=[vmem] * 7,
        out_specs=[hbm] * 5,
        scratch_shapes=[low, low, pltpu.VMEM((gain_rows, LANES), F32), dma((5,))],
        compiler_params=pltpu.CompilerParams(vmem_limit_bytes=32 * 2**20),
        name="last_products",
    )(k, v, o, gq, gk, gv, later)
    return out, gq, gk, gv, gg.reshape(width)


def solution(mesh):
    spec = P("dp", "ctx", None)
    return jax.shard_map(
        functools.partial(per_device, mesh.shape["ctx"], mesh.shape["dp"]),
        mesh=mesh,
        in_specs=(spec, spec, spec, P(), spec),
        out_specs=(spec, spec, spec, spec, P()),
        check_vma=False,
    )
```

```python
import functools

import jax
import jax.numpy as jnp
from jax import lax
from jax.experimental import pallas as pl
from jax.experimental.pallas import tpu as pltpu
from jax.sharding import PartitionSpec as P

HEAD_DIM = 64
GROUP = 128
LANES = 2 * HEAD_DIM
F32 = jnp.float32
BF16 = jnp.bfloat16
MESH = pl.DeviceIdType.MESH


def nn(a, b):
    return lax.dot_general(a, b, (((1,), (0,)), ((), ())), preferred_element_type=F32)


def nt(a, b):
    return lax.dot_general(a, b, (((1,), (1,)), ((), ())), preferred_element_type=F32)


def tn(a, b):
    return lax.dot_general(a, b, (((0,), (0,)), ((), ())), preferred_element_type=F32)


def first_head(rows):
    return lax.broadcasted_iota(jnp.int32, (rows, LANES), 1) < HEAD_DIM


def by_head(x):
    mask = first_head(x.shape[0])
    zero = jnp.zeros_like(x)
    return jnp.concatenate([jnp.where(mask, x, zero), jnp.where(mask, zero, x)], 0)


def pack(square):
    mask = first_head(HEAD_DIM)
    return jnp.where(mask, square[:HEAD_DIM], square[HEAD_DIM:])


def unpack(packed):
    mask = first_head(HEAD_DIM)
    zero = jnp.zeros_like(packed)
    both = [jnp.where(mask, packed, zero), jnp.where(mask, zero, packed)]
    return jnp.concatenate(both, 0).astype(BF16)


def side_by_side(stacked):
    return jnp.concatenate([stacked[:GROUP], stacked[GROUP:]], 1)


def flips(count):
    return sorted(range(1, count), key=lambda mask: (-(mask // 2).bit_count(), mask % 2, mask))


def flipped(place, mask, count):
    out = 0
    bit = 1
    while bit < count:
        out = out + lax.rem(place // bit + (1 if mask & bit else 0), 2) * bit
        bit *= 2
    return out


def scan_kernel(
    n, ndp, q_hbm, k_hbm, v_hbm, gain_hbm, g_hbm,
    k, v, o_out, gq_out, gk_part, gv_part, later,
    q, g, gain_ref, attn, grad_attn, scores, q_turned,
    kv, kv_in, prefix, state, qd, qd_in, suffix, sums, carry, gains,
    in_sems, send_sems, recv_sems, carry_send, carry_recv, gain_send, gain_recv,
):
    me = lax.axis_index("ctx")
    row = lax.axis_index("dp")
    width = q.shape[1]
    pairs = width // LANES
    chunks = kv.shape[0]
    group = pairs // chunks
    share = kv.shape[2]
    slots = HEAD_DIM // share
    half = n // 2
    upper = me // half
    place = lax.rem(me, half)
    other = lax.rem(me + half, n)

    barrier = pltpu.get_barrier_semaphore()
    loads = []

    def load(src, dst):
        loads.append(pltpu.make_async_copy(src, dst, in_sems.at[len(loads)]))
        loads[-1].start()

    for c in range(chunks):
        columns = slice(c * group * LANES, (c + 1) * group * LANES)
        load(k_hbm.at[0, :, columns], k.at[:, columns])
        load(v_hbm.at[0, :, columns], v.at[:, columns])

    mates = [flipped(place, mask, half) for mask in flips(half)]
    twins = [(lax.rem(row + d, ndp), c) for d in range(ndp) for c in (me, other)][1:]
    for mate in mates:
        pl.semaphore_signal(
            barrier, inc=1, device_id={"ctx": upper * half + mate}, device_id_type=MESH
        )
    for d, c in twins:
        pl.semaphore_signal(barrier, inc=1, device_id={"dp": d, "ctx": c}, device_id_type=MESH)

    def chunk(ref, c, index, extra):
        return ref.at[c, index, pl.ds(0, share + (extra if c == chunks - 1 else 0))]

    def send(phase, c, source, target, extra=0):
        for mate in mates:
            pltpu.make_async_remote_copy(
                src_ref=chunk(source, c, mate, extra),
                dst_ref=chunk(target, c, place, extra),
                send_sem=send_sems.at[phase, c],
                recv_sem=recv_sems.at[phase, c],
                device_id={"ctx": upper * half + mate},
                device_id_type=MESH,
            ).start()
        target[c, place] = source[c, place]

    def landed(phase, c, target, extra=0):
        rest = chunk(target, c, pl.ds(0, half - 1), extra)
        pltpu.make_async_copy(rest, rest, recv_sems.at[phase, c]).wait()

    def left(phase, source, extra=0):
        for c in range(chunks):
            rest = chunk(source, c, pl.ds(0, half - 1), extra)
            pltpu.make_async_copy(rest, rest, send_sems.at[phase, c]).wait()

    def carry_copy(way, c):
        return pltpu.make_async_remote_copy(
            src_ref=sums.at[way, c],
            dst_ref=carry.at[way, c],
            send_sem=carry_send.at[way, c],
            recv_sem=carry_recv.at[way, c],
            device_id={"ctx": other},
            device_id_type=MESH,
        )

    def cross(way, c, arrived, giver):
        parts = [arrived[c, j, :share] for j in range(half)]
        sums[way, c] = functools.reduce(jnp.add, parts)

        @pl.when(giver)
        def _():
            carry_copy(way, c).start()
            carry[way, c] = jnp.zeros((share, LANES), F32)

    def crossed(way, c, giver):
        @pl.when(giver)
        def _():
            carry_copy(way, c).wait_send()

        @pl.when(jnp.logical_not(giver))
        def _():
            carry_copy(way, c).wait_recv()

    def scan(way, c, arrived, result, order):
        total = carry[way, c]
        for j in order:
            result[c, j, :share] = total
            total = total + arrived[c, j, :share]

    def lanes(p):
        return slice(p * LANES, (p + 1) * LANES)

    def place_of(p):
        return p // group, p % group * HEAD_DIM // share

    def pair_of(ref, p):
        c, first = place_of(p)
        return ref[c, first : first + slots, :share].reshape(HEAD_DIM, LANES)

    def put(ref, p, packed):
        c, first = place_of(p)
        ref[c, first : first + slots, :share] = packed.reshape(slots, share, LANES)

    for c in range(chunks):
        loads[2 * c].wait()
        loads[2 * c + 1].wait()
        for p in range(c * group, (c + 1) * group):
            put(kv, p, pack(tn(k[:, lanes(p)], v[:, lanes(p)])))
        if c == 0:
            pl.semaphore_wait(barrier, len(mates) + len(twins))
        send(0, c, kv, kv_in)
    load(q_hbm.at[0], q)
    load(g_hbm.at[0], g)
    load(gain_hbm, gain_ref)

    loads[2 * chunks].wait()
    t = lax.broadcasted_iota(jnp.int32, (2 * GROUP, GROUP), 0) % GROUP
    causal = t >= lax.broadcasted_iota(jnp.int32, (2 * GROUP, GROUP), 1)

    def within(first, last):
        for p in range(pairs * first // 8, pairs * last // 8):
            s = nt(by_head(q[:, lanes(p)]), k[:, lanes(p)])
            s = jnp.where(causal, s, 0.0).astype(BF16)
            scores[p] = s
            q_turned[p] = q[:, lanes(p)].T
            attn[:, lanes(p)] = nn(side_by_side(s), by_head(v[:, lanes(p)]))

    ahead = range(half)
    lower = upper == 0
    within(0, 3)
    for c in range(chunks):
        landed(0, c, kv_in)
        cross(0, c, kv_in, lower)
    for c in range(chunks):
        crossed(0, c, lower)
        scan(0, c, kv_in, prefix, ahead)
        send(1, c, prefix, state)
    within(3, 8)
    loads[2 * chunks + 1].wait()
    loads[2 * chunks + 2].wait()

    squares = jnp.zeros((GROUP, LANES), F32)
    cross_sum = jnp.zeros((GROUP, LANES), F32)
    for c in range(chunks):
        landed(1, c, state)
        for p in range(c * group, (c + 1) * group):
            a = attn[:, lanes(p)] + nn(q[:, lanes(p)], unpack(pair_of(state, p)))
            attn[:, lanes(p)] = a
            squares += a * a
            cross_sum += a * (g[:, lanes(p)].astype(F32) * gain_ref[:, lanes(p)])
    inv = lax.rsqrt(jnp.sum(squares, 1, keepdims=True) / width + 1e-06)
    mean = jnp.sum(cross_sum, 1, keepdims=True) * inv / width
    tile = qd.shape[2] - share
    for c in range(chunks):
        for p in range(c * group, (c + 1) * group):
            normed = attn[:, lanes(p)] * inv
            gf = g[:, lanes(p)].astype(F32)
            ga = (inv * (gf * gain_ref[:, lanes(p)] - normed * mean)).astype(BF16)
            grad_attn[:, lanes(p)] = ga
            put(qd, p, pack(nn(q_turned[p], ga)))
            gain_tile = jnp.sum((gf * normed).reshape(GROUP // tile, tile, LANES), 0)
            for j in range(p * half // pairs, (p + 1) * half // pairs):
                qd[chunks - 1, j, share:] = gain_tile
        send(2, c, qd, qd_in, tile)

    def after(first, last):
        for p in range(pairs * first // 8, pairs * last // 8):
            normed = attn[:, lanes(p)] * inv
            o_out[:, lanes(p)] = (normed * gain_ref[:, lanes(p)]).astype(BF16)
            ga = grad_attn[:, lanes(p)]
            ga2 = by_head(ga)
            ds = jnp.where(causal, nt(ga2, v[:, lanes(p)]), 0.0).astype(BF16)
            gq = nn(side_by_side(ds), by_head(k[:, lanes(p)]))
            gq = gq + nt(ga, unpack(pair_of(state, p)))
            gq_out[:, lanes(p)] = gq.astype(BF16)
            gk_part[:, lanes(p)] = tn(ds, by_head(q[:, lanes(p)]))
            gv_part[:, lanes(p)] = tn(scores[p], ga2)

    back = range(half - 1, -1, -1)
    raised = upper == 1
    after(0, 2)
    for c in range(chunks):
        landed(2, c, qd_in, tile)
        cross(1, c, qd_in, raised)
    slot = 2 * row + upper
    gains[slot] = functools.reduce(jnp.add, [qd_in[chunks - 1, j, share:] for j in range(half)])
    for d, c in twins:
        pltpu.make_async_remote_copy(
            src_ref=gains.at[slot],
            dst_ref=gains.at[slot],
            send_sem=gain_send,
            recv_sem=gain_recv,
            device_id={"dp": d, "ctx": c},
            device_id_type=MESH,
        ).start()
    rest = gains.at[pl.ds(0, len(twins))]
    for c in range(chunks):
        crossed(1, c, raised)
        scan(1, c, qd_in, suffix, back)
        if c == chunks - 1:
            pltpu.make_async_copy(rest, rest, gain_recv).wait()
            gain_sum = functools.reduce(jnp.add, [gains[j] for j in range(2 * ndp)])
            for j in range(half):
                suffix[c, j, share:] = gain_sum
        send(3, c, suffix, later, tile)
    after(2, 8)

    pltpu.make_async_copy(rest, rest, gain_send).wait()
    left(0, kv)
    left(1, prefix)
    left(2, qd, tile)
    left(3, suffix, tile)
    for c in range(chunks):
        landed(3, c, later, tile)


def last_kernel(
    k, v, o, gq, gk_part, gv_part, later,
    out_hbm, gq_hbm, gk_hbm, gv_hbm, gg_hbm, gk_out, gv_out, gg, sems,
):
    stores = []

    def store(src, dst):
        stores.append(pltpu.make_async_copy(src, dst, sems.at[len(stores)]))
        stores[-1].start()

    store(o, out_hbm.at[0])
    store(gq, gq_hbm.at[0])
    width = k.shape[1]
    pairs = width // LANES
    chunks, half = later.shape[:2]
    group = pairs // chunks
    share = group * HEAD_DIM // half
    for p in range(pairs):
        gg[p : p + 1] = jnp.sum(later[chunks - 1, p * half // pairs, share:], 0, keepdims=True)
    store(gg, gg_hbm)
    for p in range(pairs):
        lanes = slice(p * LANES, (p + 1) * LANES)
        first = p % group * HEAD_DIM // share
        low = later[p // group, first : first + HEAD_DIM // share, :share]
        low = unpack(low.reshape(HEAD_DIM, LANES))
        gk_out[:, lanes] = (gk_part[:, lanes] + nt(v[:, lanes], low)).astype(BF16)
        gv_out[:, lanes] = (gv_part[:, lanes] + nn(k[:, lanes], low)).astype(BF16)
        if (p + 1) % (pairs // 2) == 0:
            done = slice((p + 1 - pairs // 2) * LANES, (p + 1) * LANES)
            store(gk_out.at[:, done], gk_hbm.at[0, :, done])
            store(gv_out.at[:, done], gv_hbm.at[0, :, done])
    for copy in stores:
        copy.wait()


def pinned(x):
    return pltpu.with_memory_space_constraint(x, pltpu.HBM)


def per_device(n, ndp, queries, keys, values, gain, grad_out):
    rows, width = queries.shape[1:]
    pairs = width // LANES
    half = n // 2
    chunks = 4 if pairs * HEAD_DIM // half >= 32 else 2
    share = pairs // chunks * HEAD_DIM // half
    gain_rows = width // LANES
    flat = jax.ShapeDtypeStruct((1, rows, width), BF16)
    low_out = jax.ShapeDtypeStruct((rows, width), BF16)
    full_out = jax.ShapeDtypeStruct((rows, width), F32)
    gain_out = jax.ShapeDtypeStruct((gain_rows, LANES), F32)
    hbm = pl.BlockSpec(memory_space=pltpu.HBM)
    vmem = pl.BlockSpec(memory_space=pltpu.VMEM)
    low = pltpu.VMEM((rows, width), BF16)
    full = pltpu.VMEM((rows, width), F32)
    part = pltpu.VMEM((chunks, half, share, LANES), F32)
    tile = 8
    wide = pltpu.VMEM((chunks, half, share + tile, LANES), F32)
    pair = pltpu.VMEM((2, chunks, share, LANES), F32)
    dma = pltpu.SemaphoreType.DMA
    k, v, o, gq, gk, gv, later = pl.pallas_call(
        functools.partial(scan_kernel, n, ndp),
        out_shape=[low_out] * 4
        + [full_out] * 2
        + [jax.ShapeDtypeStruct((chunks, half, share + tile, LANES), F32)],
        in_specs=[hbm] * 5,
        out_specs=[vmem] * 7,
        scratch_shapes=[low, low, pltpu.VMEM((1, width), F32), full, low]
        + [pltpu.VMEM((pairs, 2 * GROUP, GROUP), BF16), pltpu.VMEM((pairs, LANES, GROUP), BF16)]
        + [part] * 4
        + [wide] * 3
        + [pair, pair, pltpu.VMEM((2 * ndp, tile, LANES), F32)]
        + [dma((2 * chunks + 3,))] + [dma((4, chunks))] * 2 + [dma((2, chunks))] * 2 + [dma, dma],
        compiler_params=pltpu.CompilerParams(
            collective_id=0, has_side_effects=True, vmem_limit_bytes=32 * 2**20
        ),
        name="linear_attention",
    )(*(pinned(x) for x in (queries, keys, values, gain.reshape(1, width), grad_out)))
    out, gq, gk, gv, gg = pl.pallas_call(
        last_kernel,
        out_shape=[flat] * 4 + [gain_out],
        in_specs=[vmem] * 7,
        out_specs=[hbm] * 5,
        scratch_shapes=[low, low, pltpu.VMEM((gain_rows, LANES), F32), dma((7,))],
        compiler_params=pltpu.CompilerParams(vmem_limit_bytes=32 * 2**20),
        name="last_products",
    )(k, v, o, gq, gk, gv, later)
    return out, gq, gk, gv, gg.reshape(width)


def solution(mesh):
    spec = P("dp", "ctx", None)
    return jax.shard_map(
        functools.partial(per_device, mesh.shape["ctx"], mesh.shape["dp"]),
        mesh=mesh,
        in_specs=(spec, spec, spec, P(), spec),
        out_specs=(spec, spec, spec, spec, P()),
        check_vma=False,
    )
```

```python
import functools

import jax
import jax.numpy as jnp
from jax import lax
from jax.experimental import pallas as pl
from jax.experimental.pallas import tpu as pltpu
from jax.sharding import PartitionSpec as P

HEAD_DIM = 64
GROUP = 128
LANES = 2 * HEAD_DIM
F32 = jnp.float32
BF16 = jnp.bfloat16
MESH = pl.DeviceIdType.MESH


def nn(a, b):
    return lax.dot_general(a, b, (((1,), (0,)), ((), ())), preferred_element_type=F32)


def nt(a, b):
    return lax.dot_general(a, b, (((1,), (1,)), ((), ())), preferred_element_type=F32)


def tn(a, b):
    return lax.dot_general(a, b, (((0,), (0,)), ((), ())), preferred_element_type=F32)


def first_head(rows):
    return lax.broadcasted_iota(jnp.int32, (rows, LANES), 1) < HEAD_DIM


def by_head(x):
    mask = first_head(x.shape[0])
    zero = jnp.zeros_like(x)
    return jnp.concatenate([jnp.where(mask, x, zero), jnp.where(mask, zero, x)], 0)


def pack(square):
    mask = first_head(HEAD_DIM)
    return jnp.where(mask, square[:HEAD_DIM], square[HEAD_DIM:])


def unpack(packed):
    mask = first_head(HEAD_DIM)
    zero = jnp.zeros_like(packed)
    both = [jnp.where(mask, packed, zero), jnp.where(mask, zero, packed)]
    return jnp.concatenate(both, 0).astype(BF16)


def side_by_side(stacked):
    return jnp.concatenate([stacked[:GROUP], stacked[GROUP:]], 1)


def flips(count):
    return sorted(range(1, count), key=lambda mask: (-(mask // 2).bit_count(), mask % 2, mask))


def flipped(place, mask, count):
    out = 0
    bit = 1
    while bit < count:
        out = out + lax.rem(place // bit + (1 if mask & bit else 0), 2) * bit
        bit *= 2
    return out


def scan_kernel(
    n, ndp, q_hbm, k_hbm, v_hbm, gain_hbm, g_hbm,
    o_out, gq_out, gk_out, gv_out, gg_out,
    k, v, q, g, gain_ref, attn, grad_attn, scores, q_turned, gk_part, gv_part,
    kv, kv_in, prefix, state, qd, qd_in, suffix, later, sums, carry, gains,
    in_sems, send_sems, recv_sems, carry_send, carry_recv, gain_send, gain_recv,
):
    me = lax.axis_index("ctx")
    row = lax.axis_index("dp")
    width = q.shape[1]
    pairs = width // LANES
    chunks = kv.shape[0]
    group = pairs // chunks
    share = kv.shape[2]
    slots = HEAD_DIM // share
    half = n // 2
    upper = me // half
    place = lax.rem(me, half)
    other = lax.rem(me + half, n)

    barrier = pltpu.get_barrier_semaphore()
    loads = []

    def load(src, dst):
        loads.append(pltpu.make_async_copy(src, dst, in_sems.at[len(loads)]))
        loads[-1].start()

    for c in range(chunks):
        columns = slice(c * group * LANES, (c + 1) * group * LANES)
        load(k_hbm.at[0, :, columns], k.at[:, columns])
        load(v_hbm.at[0, :, columns], v.at[:, columns])

    mates = [flipped(place, mask, half) for mask in flips(half)]
    twins = [(lax.rem(row + d, ndp), c) for d in range(ndp) for c in (me, other)][1:]
    for mate in mates:
        pl.semaphore_signal(
            barrier, inc=1, device_id={"ctx": upper * half + mate}, device_id_type=MESH
        )
    for d, c in twins:
        pl.semaphore_signal(barrier, inc=1, device_id={"dp": d, "ctx": c}, device_id_type=MESH)

    def chunk(ref, c, index, extra):
        return ref.at[c, index, pl.ds(0, share + (extra if c == chunks - 1 else 0))]

    def send(phase, c, source, target, extra=0):
        for mate in mates:
            pltpu.make_async_remote_copy(
                src_ref=chunk(source, c, mate, extra),
                dst_ref=chunk(target, c, place, extra),
                send_sem=send_sems.at[phase, c],
                recv_sem=recv_sems.at[phase, c],
                device_id={"ctx": upper * half + mate},
                device_id_type=MESH,
            ).start()
        target[c, place] = source[c, place]

    def landed(phase, c, target, extra=0):
        rest = chunk(target, c, pl.ds(0, half - 1), extra)
        pltpu.make_async_copy(rest, rest, recv_sems.at[phase, c]).wait()

    pending = []

    def left(phase, c, source, extra=0):
        rest = chunk(source, c, pl.ds(0, half - 1), extra)
        pltpu.make_async_copy(rest, rest, send_sems.at[phase, c]).wait()

    def paced(phase, c, source, target, extra=0):
        if c >= 2:
            left(*pending.pop(0))
        send(phase, c, source, target, extra)
        pending.append((phase, c, source, extra))

    def flush():
        while pending:
            left(*pending.pop(0))

    def carry_copy(way, c):
        return pltpu.make_async_remote_copy(
            src_ref=sums.at[way, c],
            dst_ref=carry.at[way, c],
            send_sem=carry_send.at[way, c],
            recv_sem=carry_recv.at[way, c],
            device_id={"ctx": other},
            device_id_type=MESH,
        )

    def cross(way, c, arrived, giver):
        parts = [arrived[c, j, :share] for j in range(half)]
        sums[way, c] = functools.reduce(jnp.add, parts)

        @pl.when(giver)
        def _():
            carry_copy(way, c).start()
            carry[way, c] = jnp.zeros((share, LANES), F32)

    def crossed(way, c, giver):
        @pl.when(giver)
        def _():
            carry_copy(way, c).wait_send()

        @pl.when(jnp.logical_not(giver))
        def _():
            carry_copy(way, c).wait_recv()

    def scan(way, c, arrived, result, order):
        total = carry[way, c]
        for j in order:
            result[c, j, :share] = total
            total = total + arrived[c, j, :share]

    def lanes(p):
        return slice(p * LANES, (p + 1) * LANES)

    def place_of(p):
        return p // group, p % group * HEAD_DIM // share

    def pair_of(ref, p):
        c, first = place_of(p)
        return ref[c, first : first + slots, :share].reshape(HEAD_DIM, LANES)

    def put(ref, p, packed):
        c, first = place_of(p)
        ref[c, first : first + slots, :share] = packed.reshape(slots, share, LANES)

    for c in range(chunks):
        loads[2 * c].wait()
        loads[2 * c + 1].wait()
        for p in range(c * group, (c + 1) * group):
            put(kv, p, pack(tn(k[:, lanes(p)], v[:, lanes(p)])))
        if c == 0:
            pl.semaphore_wait(barrier, len(mates) + len(twins))
        paced(0, c, kv, kv_in)
    load(q_hbm.at[0], q)
    load(g_hbm.at[0], g)
    load(gain_hbm, gain_ref)

    loads[2 * chunks].wait()
    t = lax.broadcasted_iota(jnp.int32, (2 * GROUP, GROUP), 0) % GROUP
    causal = t >= lax.broadcasted_iota(jnp.int32, (2 * GROUP, GROUP), 1)

    def within(first, last):
        for p in range(pairs * first // 8, pairs * last // 8):
            s = nt(by_head(q[:, lanes(p)]), k[:, lanes(p)])
            s = jnp.where(causal, s, 0.0).astype(BF16)
            scores[p] = s
            q_turned[p] = q[:, lanes(p)].T
            attn[:, lanes(p)] = nn(side_by_side(s), by_head(v[:, lanes(p)]))

    ahead = range(half)
    lower = upper == 0
    within(0, 3)
    for c in range(chunks):
        landed(0, c, kv_in)
        cross(0, c, kv_in, lower)
    flush()
    for c in range(chunks):
        crossed(0, c, lower)
        scan(0, c, kv_in, prefix, ahead)
        paced(1, c, prefix, state)
    within(3, 8)
    loads[2 * chunks + 1].wait()
    loads[2 * chunks + 2].wait()

    squares = jnp.zeros((GROUP, LANES), F32)
    cross_sum = jnp.zeros((GROUP, LANES), F32)
    for c in range(chunks):
        landed(1, c, state)
        for p in range(c * group, (c + 1) * group):
            a = attn[:, lanes(p)] + nn(q[:, lanes(p)], unpack(pair_of(state, p)))
            attn[:, lanes(p)] = a
            squares += a * a
            cross_sum += a * (g[:, lanes(p)].astype(F32) * gain_ref[:, lanes(p)])
    inv = lax.rsqrt(jnp.sum(squares, 1, keepdims=True) / width + 1e-06)
    mean = jnp.sum(cross_sum, 1, keepdims=True) * inv / width
    flush()
    tile = qd.shape[2] - share
    for c in range(chunks):
        for p in range(c * group, (c + 1) * group):
            normed = attn[:, lanes(p)] * inv
            gf = g[:, lanes(p)].astype(F32)
            ga = (inv * (gf * gain_ref[:, lanes(p)] - normed * mean)).astype(BF16)
            grad_attn[:, lanes(p)] = ga
            put(qd, p, pack(nn(q_turned[p], ga)))
            gain_tile = jnp.sum((gf * normed).reshape(GROUP // tile, tile, LANES), 0)
            for j in range(p * half // pairs, (p + 1) * half // pairs):
                qd[chunks - 1, j, share:] = gain_tile
        if c < 2:
            paced(2, c, qd, qd_in, tile)
    for c in range(2, chunks):
        paced(2, c, qd, qd_in, tile)

    def after(first, last):
        for p in range(pairs * first // 8, pairs * last // 8):
            normed = attn[:, lanes(p)] * inv
            o_out[:, lanes(p)] = (normed * gain_ref[:, lanes(p)]).astype(BF16)
            ga = grad_attn[:, lanes(p)]
            ga2 = by_head(ga)
            ds = jnp.where(causal, nt(ga2, v[:, lanes(p)]), 0.0).astype(BF16)
            gq = nn(side_by_side(ds), by_head(k[:, lanes(p)]))
            gq = gq + nt(ga, unpack(pair_of(state, p)))
            gq_out[:, lanes(p)] = gq.astype(BF16)
            gk_part[:, lanes(p)] = tn(ds, by_head(q[:, lanes(p)]))
            gv_part[:, lanes(p)] = tn(scores[p], ga2)

    back = range(half - 1, -1, -1)
    raised = upper == 1
    after(0, 2)
    for c in range(chunks):
        landed(2, c, qd_in, tile)
        cross(1, c, qd_in, raised)
    slot = 2 * row + upper
    gains[slot] = functools.reduce(jnp.add, [qd_in[chunks - 1, j, share:] for j in range(half)])
    for d, c in twins:
        pltpu.make_async_remote_copy(
            src_ref=gains.at[slot],
            dst_ref=gains.at[slot],
            send_sem=gain_send,
            recv_sem=gain_recv,
            device_id={"dp": d, "ctx": c},
            device_id_type=MESH,
        ).start()
    flush()
    rest = gains.at[pl.ds(0, len(twins))]
    for c in range(chunks):
        crossed(1, c, raised)
        scan(1, c, qd_in, suffix, back)
        if c == chunks - 1:
            pltpu.make_async_copy(rest, rest, gain_recv).wait()
            gain_sum = functools.reduce(jnp.add, [gains[j] for j in range(2 * ndp)])
            for j in range(half):
                suffix[c, j, share:] = gain_sum
        paced(3, c, suffix, later, tile)
    after(2, 8)

    pltpu.make_async_copy(rest, rest, gain_send).wait()
    flush()
    for c in range(chunks):
        landed(3, c, later, tile)
        for p in range(c * group, (c + 1) * group):
            low = unpack(pair_of(later, p))
            gk = gk_part[:, lanes(p)] + nt(v[:, lanes(p)], low)
            gv = gv_part[:, lanes(p)] + nn(k[:, lanes(p)], low)
            gk_out[:, lanes(p)] = gk.astype(BF16)
            gv_out[:, lanes(p)] = gv.astype(BF16)
    for p in range(pairs):
        gain_rows = later[chunks - 1, p * half // pairs, share:]
        gg_out[p : p + 1] = jnp.sum(gain_rows, 0, keepdims=True)


def last_kernel(o, gq, gk, gv, gg, out_hbm, gq_hbm, gk_hbm, gv_hbm, gg_hbm, sems):
    stores = []
    arrays = (o, out_hbm.at[0]), (gq, gq_hbm.at[0]), (gk, gk_hbm.at[0]), (gv, gv_hbm.at[0])
    for i, (src, dst) in enumerate(arrays + ((gg, gg_hbm),)):
        stores.append(pltpu.make_async_copy(src, dst, sems.at[i]))
        stores[-1].start()
    for copy in stores:
        copy.wait()


def pinned(x):
    return pltpu.with_memory_space_constraint(x, pltpu.HBM)


def per_device(n, ndp, queries, keys, values, gain, grad_out):
    rows, width = queries.shape[1:]
    pairs = width // LANES
    half = n // 2
    chunks = 4 if pairs * HEAD_DIM // half >= 32 else 2
    share = pairs // chunks * HEAD_DIM // half
    gain_rows = width // LANES
    flat = jax.ShapeDtypeStruct((1, rows, width), BF16)
    low_out = jax.ShapeDtypeStruct((rows, width), BF16)
    gain_out = jax.ShapeDtypeStruct((gain_rows, LANES), F32)
    hbm = pl.BlockSpec(memory_space=pltpu.HBM)
    vmem = pl.BlockSpec(memory_space=pltpu.VMEM)
    low = pltpu.VMEM((rows, width), BF16)
    full = pltpu.VMEM((rows, width), F32)
    part = pltpu.VMEM((chunks, half, share, LANES), F32)
    tile = 8
    wide = pltpu.VMEM((chunks, half, share + tile, LANES), F32)
    pair = pltpu.VMEM((2, chunks, share, LANES), F32)
    dma = pltpu.SemaphoreType.DMA
    results = pl.pallas_call(
        functools.partial(scan_kernel, n, ndp),
        out_shape=[low_out] * 4 + [gain_out],
        in_specs=[hbm] * 5,
        out_specs=[vmem] * 5,
        scratch_shapes=[low] * 4
        + [pltpu.VMEM((1, width), F32), full, low, pltpu.VMEM((pairs, 2 * GROUP, GROUP), BF16)]
        + [pltpu.VMEM((pairs, LANES, GROUP), BF16), full, full]
        + [part] * 4
        + [wide] * 4
        + [pair, pair, pltpu.VMEM((2 * ndp, tile, LANES), F32)]
        + [dma((2 * chunks + 3,))]
        + [dma((4, chunks))] * 2
        + [dma((2, chunks))] * 2
        + [dma, dma],
        compiler_params=pltpu.CompilerParams(
            collective_id=0, has_side_effects=True, vmem_limit_bytes=32 * 2**20
        ),
        name="linear_attention",
    )(*(pinned(x) for x in (queries, keys, values, gain.reshape(1, width), grad_out)))
    out, gq, gk, gv, gg = pl.pallas_call(
        last_kernel,
        out_shape=[flat] * 4 + [gain_out],
        in_specs=[vmem] * 5,
        out_specs=[hbm] * 5,
        scratch_shapes=[dma((5,))],
        compiler_params=pltpu.CompilerParams(vmem_limit_bytes=32 * 2**20),
        name="store_results",
    )(*results)
    return out, gq, gk, gv, gg.reshape(width)


def solution(mesh):
    spec = P("dp", "ctx", None)
    return jax.shard_map(
        functools.partial(per_device, mesh.shape["ctx"], mesh.shape["dp"]),
        mesh=mesh,
        in_specs=(spec, spec, spec, P(), spec),
        out_specs=(spec, spec, spec, spec, P()),
        check_vma=False,
    )
```

```python
import functools

import jax
import jax.numpy as jnp
from jax import lax
from jax.experimental import pallas as pl
from jax.experimental.pallas import tpu as pltpu
from jax.sharding import PartitionSpec as P

HEAD_DIM = 64
GROUP = 128
LANES = 2 * HEAD_DIM
F32 = jnp.float32
BF16 = jnp.bfloat16
MESH = pl.DeviceIdType.MESH


def nn(a, b):
    return lax.dot_general(a, b, (((1,), (0,)), ((), ())), preferred_element_type=F32)


def nt(a, b):
    return lax.dot_general(a, b, (((1,), (1,)), ((), ())), preferred_element_type=F32)


def tn(a, b):
    return lax.dot_general(a, b, (((0,), (0,)), ((), ())), preferred_element_type=F32)


def first_head(rows):
    return lax.broadcasted_iota(jnp.int32, (rows, LANES), 1) < HEAD_DIM


def by_head(x):
    mask = first_head(x.shape[0])
    zero = jnp.zeros_like(x)
    return jnp.concatenate([jnp.where(mask, x, zero), jnp.where(mask, zero, x)], 0)


def pack(square):
    mask = first_head(HEAD_DIM)
    return jnp.where(mask, square[:HEAD_DIM], square[HEAD_DIM:])


def unpack(packed):
    mask = first_head(HEAD_DIM)
    zero = jnp.zeros_like(packed)
    both = [jnp.where(mask, packed, zero), jnp.where(mask, zero, packed)]
    return jnp.concatenate(both, 0).astype(BF16)


def side_by_side(stacked):
    return jnp.concatenate([stacked[:GROUP], stacked[GROUP:]], 1)


def flips(count):
    return sorted(range(1, count), key=lambda mask: (-(mask // 2).bit_count(), mask % 2, mask))


def flipped(place, mask, count):
    out = 0
    bit = 1
    while bit < count:
        out = out + lax.rem(place // bit + (1 if mask & bit else 0), 2) * bit
        bit *= 2
    return out


def scan_kernel(
    n, ndp, q_hbm, k_hbm, v_hbm, gain_hbm, g_hbm,
    k, v, o_out, gq_out, gk_part, gv_part, later,
    q, g, gain_ref, attn, grad_attn, scores, q_turned,
    kv, kv_in, prefix, state, qd, qd_in, suffix, sums, carry, gains,
    in_sems, send_sems, recv_sems, carry_send, carry_recv, gain_send, gain_recv,
):
    me = lax.axis_index("ctx")
    row = lax.axis_index("dp")
    width = q.shape[1]
    pairs = width // LANES
    chunks = kv.shape[0]
    group = pairs // chunks
    share = kv.shape[2]
    slots = HEAD_DIM // share
    half = n // 2
    upper = me // half
    place = lax.rem(me, half)
    other = lax.rem(me + half, n)

    barrier = pltpu.get_barrier_semaphore()
    mates = [flipped(place, mask, half) for mask in flips(half)]
    twins = [(lax.rem(row + d, ndp), c) for d in range(ndp) for c in (me, other)][1:]
    for mate in mates:
        pl.semaphore_signal(
            barrier, inc=1, device_id={"ctx": upper * half + mate}, device_id_type=MESH
        )
    for d, c in twins:
        pl.semaphore_signal(barrier, inc=1, device_id={"dp": d, "ctx": c}, device_id_type=MESH)

    loads = []

    def load(src, dst):
        loads.append(pltpu.make_async_copy(src, dst, in_sems.at[len(loads)]))
        loads[-1].start()

    for c in range(chunks):
        columns = slice(c * group * LANES, (c + 1) * group * LANES)
        load(k_hbm.at[0, :, columns], k.at[:, columns])
        load(v_hbm.at[0, :, columns], v.at[:, columns])

    def chunk(ref, c, index, extra):
        return ref.at[c, index, pl.ds(0, share + (extra if c == chunks - 1 else 0))]

    def send(phase, c, source, target, extra=0):
        for mate in mates:
            pltpu.make_async_remote_copy(
                src_ref=chunk(source, c, mate, extra),
                dst_ref=chunk(target, c, place, extra),
                send_sem=send_sems.at[phase, c],
                recv_sem=recv_sems.at[phase, c],
                device_id={"ctx": upper * half + mate},
                device_id_type=MESH,
            ).start()
        target[c, place] = source[c, place]

    def landed(phase, c, target, extra=0):
        rest = chunk(target, c, pl.ds(0, half - 1), extra)
        pltpu.make_async_copy(rest, rest, recv_sems.at[phase, c]).wait()

    def left(phase, source, extra=0):
        for c in range(chunks):
            rest = chunk(source, c, pl.ds(0, half - 1), extra)
            pltpu.make_async_copy(rest, rest, send_sems.at[phase, c]).wait()

    def carry_copy(way, c):
        return pltpu.make_async_remote_copy(
            src_ref=sums.at[way, c],
            dst_ref=carry.at[way, c],
            send_sem=carry_send.at[way, c],
            recv_sem=carry_recv.at[way, c],
            device_id={"ctx": other},
            device_id_type=MESH,
        )

    def cross(way, c, arrived, giver):
        parts = [arrived[c, j, :share] for j in range(half)]
        sums[way, c] = functools.reduce(jnp.add, parts)

        @pl.when(giver)
        def _():
            carry_copy(way, c).start()
            carry[way, c] = jnp.zeros((share, LANES), F32)

    def crossed(way, c, giver):
        @pl.when(giver)
        def _():
            carry_copy(way, c).wait_send()

        @pl.when(jnp.logical_not(giver))
        def _():
            carry_copy(way, c).wait_recv()

    def scan(way, c, arrived, result, order):
        total = carry[way, c]
        for j in order:
            result[c, j, :share] = total
            total = total + arrived[c, j, :share]

    def lanes(p):
        return slice(p * LANES, (p + 1) * LANES)

    def place_of(p):
        return p // group, p % group * HEAD_DIM // share

    def pair_of(ref, p):
        c, first = place_of(p)
        return ref[c, first : first + slots, :share].reshape(HEAD_DIM, LANES)

    def put(ref, p, packed):
        c, first = place_of(p)
        ref[c, first : first + slots, :share] = packed.reshape(slots, share, LANES)

    for c in range(chunks):
        loads[2 * c].wait()
        loads[2 * c + 1].wait()
        for p in range(c * group, (c + 1) * group):
            put(kv, p, pack(tn(k[:, lanes(p)], v[:, lanes(p)])))
        if c == 0:
            pl.semaphore_wait(barrier, len(mates) + len(twins))
        send(0, c, kv, kv_in)
    load(q_hbm.at[0], q)
    load(g_hbm.at[0], g)
    load(gain_hbm, gain_ref)

    loads[2 * chunks].wait()
    t = lax.broadcasted_iota(jnp.int32, (2 * GROUP, GROUP), 0) % GROUP
    causal = t >= lax.broadcasted_iota(jnp.int32, (2 * GROUP, GROUP), 1)

    def within(first, last):
        for p in range(pairs * first // 8, pairs * last // 8):
            s = nt(by_head(q[:, lanes(p)]), k[:, lanes(p)])
            s = jnp.where(causal, s, 0.0).astype(BF16)
            scores[p] = s
            q_turned[p] = q[:, lanes(p)].T
            attn[:, lanes(p)] = nn(side_by_side(s), by_head(v[:, lanes(p)]))

    ahead = range(half)
    lower = upper == 0
    within(0, 3)
    for c in range(chunks):
        landed(0, c, kv_in)
        cross(0, c, kv_in, lower)
    for c in range(chunks):
        crossed(0, c, lower)
        scan(0, c, kv_in, prefix, ahead)
        send(1, c, prefix, state)
    within(3, 8)
    loads[2 * chunks + 1].wait()
    loads[2 * chunks + 2].wait()

    squares = jnp.zeros((GROUP, LANES), F32)
    cross_sum = jnp.zeros((GROUP, LANES), F32)
    for c in range(chunks):
        landed(1, c, state)
        for p in range(c * group, (c + 1) * group):
            a = attn[:, lanes(p)] + nn(q[:, lanes(p)], unpack(pair_of(state, p)))
            attn[:, lanes(p)] = a
            squares += a * a
            cross_sum += a * (g[:, lanes(p)].astype(F32) * gain_ref[:, lanes(p)])
    inv = lax.rsqrt(jnp.sum(squares, 1, keepdims=True) / width + 1e-06)
    mean = jnp.sum(cross_sum, 1, keepdims=True) * inv / width
    tile = qd.shape[2] - share
    for c in range(chunks):
        for p in range(c * group, (c + 1) * group):
            normed = attn[:, lanes(p)] * inv
            gf = g[:, lanes(p)].astype(F32)
            ga = (inv * (gf * gain_ref[:, lanes(p)] - normed * mean)).astype(BF16)
            grad_attn[:, lanes(p)] = ga
            put(qd, p, pack(nn(q_turned[p], ga)))
            gain_tile = jnp.sum((gf * normed).reshape(GROUP // tile, tile, LANES), 0)
            for j in range(p * half // pairs, (p + 1) * half // pairs):
                qd[chunks - 1, j, share:] = gain_tile
        send(2, c, qd, qd_in, tile)

    def after(first, last):
        for p in range(pairs * first // 8, pairs * last // 8):
            normed = attn[:, lanes(p)] * inv
            o_out[:, lanes(p)] = (normed * gain_ref[:, lanes(p)]).astype(BF16)
            ga = grad_attn[:, lanes(p)]
            ga2 = by_head(ga)
            ds = jnp.where(causal, nt(ga2, v[:, lanes(p)]), 0.0).astype(BF16)
            gq = nn(side_by_side(ds), by_head(k[:, lanes(p)]))
            gq = gq + nt(ga, unpack(pair_of(state, p)))
            gq_out[:, lanes(p)] = gq.astype(BF16)
            gk_part[:, lanes(p)] = tn(ds, by_head(q[:, lanes(p)]))
            gv_part[:, lanes(p)] = tn(scores[p], ga2)

    back = range(half - 1, -1, -1)
    raised = upper == 1
    after(0, 2)
    for c in range(chunks):
        landed(2, c, qd_in, tile)
        cross(1, c, qd_in, raised)
    slot = 2 * row + upper
    gains[slot] = functools.reduce(jnp.add, [qd_in[chunks - 1, j, share:] for j in range(half)])
    for d, c in twins:
        pltpu.make_async_remote_copy(
            src_ref=gains.at[slot],
            dst_ref=gains.at[slot],
            send_sem=gain_send,
            recv_sem=gain_recv,
            device_id={"dp": d, "ctx": c},
            device_id_type=MESH,
        ).start()
    rest = gains.at[pl.ds(0, len(twins))]
    for c in range(chunks):
        crossed(1, c, raised)
        scan(1, c, qd_in, suffix, back)
        if c == chunks - 1:
            pltpu.make_async_copy(rest, rest, gain_recv).wait()
            gain_sum = functools.reduce(jnp.add, [gains[j] for j in range(2 * ndp)])
            for j in range(half):
                suffix[c, j, share:] = gain_sum
        send(3, c, suffix, later, tile)
    after(2, 8)

    pltpu.make_async_copy(rest, rest, gain_send).wait()
    left(0, kv)
    left(1, prefix)
    left(2, qd, tile)
    left(3, suffix, tile)
    for c in range(chunks):
        landed(3, c, later, tile)


def last_kernel(
    k, v, o, gq, gk_part, gv_part, later,
    out_hbm, gq_hbm, gk_hbm, gv_hbm, gg_hbm, gk_out, gv_out, gg, sems,
):
    stores = []

    def store(src, dst):
        stores.append(pltpu.make_async_copy(src, dst, sems.at[len(stores)]))
        stores[-1].start()

    store(o, out_hbm.at[0])
    store(gq, gq_hbm.at[0])
    width = k.shape[1]
    pairs = width // LANES
    chunks, half = later.shape[:2]
    group = pairs // chunks
    share = group * HEAD_DIM // half
    for p in range(pairs):
        gg[p : p + 1] = jnp.sum(later[chunks - 1, p * half // pairs, share:], 0, keepdims=True)
    store(gg, gg_hbm)
    for p in range(pairs):
        lanes = slice(p * LANES, (p + 1) * LANES)
        first = p % group * HEAD_DIM // share
        low = later[p // group, first : first + HEAD_DIM // share, :share]
        low = unpack(low.reshape(HEAD_DIM, LANES))
        gk_out[:, lanes] = (gk_part[:, lanes] + nt(v[:, lanes], low)).astype(BF16)
        gv_out[:, lanes] = (gv_part[:, lanes] + nn(k[:, lanes], low)).astype(BF16)
        if (p + 1) % (pairs // 2) == 0:
            done = slice((p + 1 - pairs // 2) * LANES, (p + 1) * LANES)
            store(gk_out.at[:, done], gk_hbm.at[0, :, done])
            store(gv_out.at[:, done], gv_hbm.at[0, :, done])
    for copy in stores:
        copy.wait()


def pinned(x):
    return pltpu.with_memory_space_constraint(x, pltpu.HBM)


def per_device(n, ndp, queries, keys, values, gain, grad_out):
    rows, width = queries.shape[1:]
    pairs = width // LANES
    half = n // 2
    chunks = 2
    share = pairs // chunks * HEAD_DIM // half
    gain_rows = width // LANES
    flat = jax.ShapeDtypeStruct((1, rows, width), BF16)
    low_out = jax.ShapeDtypeStruct((rows, width), BF16)
    full_out = jax.ShapeDtypeStruct((rows, width), F32)
    gain_out = jax.ShapeDtypeStruct((gain_rows, LANES), F32)
    hbm = pl.BlockSpec(memory_space=pltpu.HBM)
    vmem = pl.BlockSpec(memory_space=pltpu.VMEM)
    low = pltpu.VMEM((rows, width), BF16)
    full = pltpu.VMEM((rows, width), F32)
    part = pltpu.VMEM((chunks, half, share, LANES), F32)
    tile = 8
    wide = pltpu.VMEM((chunks, half, share + tile, LANES), F32)
    pair = pltpu.VMEM((2, chunks, share, LANES), F32)
    dma = pltpu.SemaphoreType.DMA
    k, v, o, gq, gk, gv, later = pl.pallas_call(
        functools.partial(scan_kernel, n, ndp),
        out_shape=[low_out] * 4
        + [full_out] * 2
        + [jax.ShapeDtypeStruct((chunks, half, share + tile, LANES), F32)],
        in_specs=[hbm] * 5,
        out_specs=[vmem] * 7,
        scratch_shapes=[low, low, pltpu.VMEM((1, width), F32), full, low]
        + [pltpu.VMEM((pairs, 2 * GROUP, GROUP), BF16), pltpu.VMEM((pairs, LANES, GROUP), BF16)]
        + [part] * 4
        + [wide] * 3
        + [pair, pair, pltpu.VMEM((2 * ndp, tile, LANES), F32)]
        + [dma((2 * chunks + 3,))] + [dma((4, chunks))] * 2 + [dma((2, chunks))] * 2 + [dma, dma],
        compiler_params=pltpu.CompilerParams(
            collective_id=0, has_side_effects=True, vmem_limit_bytes=32 * 2**20
        ),
        name="linear_attention",
    )(*(pinned(x) for x in (queries, keys, values, gain.reshape(1, width), grad_out)))
    out, gq, gk, gv, gg = pl.pallas_call(
        last_kernel,
        out_shape=[flat] * 4 + [gain_out],
        in_specs=[vmem] * 7,
        out_specs=[hbm] * 5,
        scratch_shapes=[low, low, pltpu.VMEM((gain_rows, LANES), F32), dma((7,))],
        compiler_params=pltpu.CompilerParams(vmem_limit_bytes=32 * 2**20),
        name="last_products",
    )(k, v, o, gq, gk, gv, later)
    return out, gq, gk, gv, gg.reshape(width)


def solution(mesh):
    spec = P("dp", "ctx", None)
    return jax.shard_map(
        functools.partial(per_device, mesh.shape["ctx"], mesh.shape["dp"]),
        mesh=mesh,
        in_specs=(spec, spec, spec, P(), spec),
        out_specs=(spec, spec, spec, spec, P()),
        check_vma=False,
    )
```

```python
import functools

import jax
import jax.numpy as jnp
from jax import lax
from jax.experimental import pallas as pl
from jax.experimental.pallas import tpu as pltpu
from jax.sharding import PartitionSpec as P

HEAD_DIM = 64
GROUP = 128
LANES = 2 * HEAD_DIM
F32 = jnp.float32
BF16 = jnp.bfloat16
MESH = pl.DeviceIdType.MESH


def nn(a, b):
    return lax.dot_general(a, b, (((1,), (0,)), ((), ())), preferred_element_type=F32)


def nt(a, b):
    return lax.dot_general(a, b, (((1,), (1,)), ((), ())), preferred_element_type=F32)


def tn(a, b):
    return lax.dot_general(a, b, (((0,), (0,)), ((), ())), preferred_element_type=F32)


def first_head(rows):
    return lax.broadcasted_iota(jnp.int32, (rows, LANES), 1) < HEAD_DIM


def by_head(x):
    mask = first_head(x.shape[0])
    zero = jnp.zeros_like(x)
    return jnp.concatenate([jnp.where(mask, x, zero), jnp.where(mask, zero, x)], 0)


def pack(square):
    mask = first_head(HEAD_DIM)
    return jnp.where(mask, square[:HEAD_DIM], square[HEAD_DIM:])


def unpack(packed):
    mask = first_head(HEAD_DIM)
    zero = jnp.zeros_like(packed)
    both = [jnp.where(mask, packed, zero), jnp.where(mask, zero, packed)]
    return jnp.concatenate(both, 0).astype(BF16)


def side_by_side(stacked):
    return jnp.concatenate([stacked[:GROUP], stacked[GROUP:]], 1)


def flips(count):
    return sorted(range(1, count), key=lambda mask: (-(mask // 2).bit_count(), mask % 2, mask))


def flipped(place, mask, count):
    out = 0
    bit = 1
    while bit < count:
        out = out + lax.rem(place // bit + (1 if mask & bit else 0), 2) * bit
        bit *= 2
    return out


def scan_kernel(
    n, ndp, q_hbm, k_hbm, v_hbm, gain_hbm, g_hbm,
    k, v, o_out, gq_out, gk_part, gv_part, later,
    q, g, gain_ref, attn, grad_attn, scores, q_turned, grad_norm,
    kv, kv_in, prefix, state, qd, qd_in, suffix, sums, carry, gains,
    in_sems, send_sems, recv_sems, carry_send, carry_recv, gain_send, gain_recv,
):
    me = lax.axis_index("ctx")
    row = lax.axis_index("dp")
    width = q.shape[1]
    pairs = width // LANES
    chunks = kv.shape[0]
    group = pairs // chunks
    share = kv.shape[2]
    slots = HEAD_DIM // share
    half = n // 2
    upper = me // half
    place = lax.rem(me, half)
    other = lax.rem(me + half, n)

    barrier = pltpu.get_barrier_semaphore()
    mates = [flipped(place, mask, half) for mask in flips(half)]
    twins = [(lax.rem(row + d, ndp), c) for d in range(ndp) for c in (me, other)][1:]
    for mate in mates:
        pl.semaphore_signal(
            barrier, inc=1, device_id={"ctx": upper * half + mate}, device_id_type=MESH
        )
    for d, c in twins:
        pl.semaphore_signal(barrier, inc=1, device_id={"dp": d, "ctx": c}, device_id_type=MESH)

    loads = []

    def load(src, dst):
        loads.append(pltpu.make_async_copy(src, dst, in_sems.at[len(loads)]))
        loads[-1].start()

    for c in range(chunks):
        columns = slice(c * group * LANES, (c + 1) * group * LANES)
        load(k_hbm.at[0, :, columns], k.at[:, columns])
        load(v_hbm.at[0, :, columns], v.at[:, columns])

    def chunk(ref, c, index, extra):
        return ref.at[c, index, pl.ds(0, share + (extra if c == chunks - 1 else 0))]

    def send(phase, c, source, target, extra=0):
        for mate in mates:
            pltpu.make_async_remote_copy(
                src_ref=chunk(source, c, mate, extra),
                dst_ref=chunk(target, c, place, extra),
                send_sem=send_sems.at[phase, c],
                recv_sem=recv_sems.at[phase, c],
                device_id={"ctx": upper * half + mate},
                device_id_type=MESH,
            ).start()
        target[c, place] = source[c, place]

    def landed(phase, c, target, extra=0):
        rest = chunk(target, c, pl.ds(0, half - 1), extra)
        pltpu.make_async_copy(rest, rest, recv_sems.at[phase, c]).wait()

    def left(phase, source, extra=0):
        for c in range(chunks):
            rest = chunk(source, c, pl.ds(0, half - 1), extra)
            pltpu.make_async_copy(rest, rest, send_sems.at[phase, c]).wait()

    def carry_copy(way, c):
        return pltpu.make_async_remote_copy(
            src_ref=sums.at[way, c],
            dst_ref=carry.at[way, c],
            send_sem=carry_send.at[way, c],
            recv_sem=carry_recv.at[way, c],
            device_id={"ctx": other},
            device_id_type=MESH,
        )

    def cross(way, c, arrived, giver):
        parts = [arrived[c, j, :share] for j in range(half)]
        sums[way, c] = functools.reduce(jnp.add, parts)

        @pl.when(giver)
        def _():
            carry_copy(way, c).start()
            carry[way, c] = jnp.zeros((share, LANES), F32)

    def crossed(way, c, giver):
        @pl.when(giver)
        def _():
            carry_copy(way, c).wait_send()

        @pl.when(jnp.logical_not(giver))
        def _():
            carry_copy(way, c).wait_recv()

    def scan(way, c, arrived, result, order):
        total = carry[way, c]
        for j in order:
            result[c, j, :share] = total
            total = total + arrived[c, j, :share]

    def lanes(p):
        return slice(p * LANES, (p + 1) * LANES)

    def place_of(p):
        return p // group, p % group * HEAD_DIM // share

    def pair_of(ref, p):
        c, first = place_of(p)
        return ref[c, first : first + slots, :share].reshape(HEAD_DIM, LANES)

    def put(ref, p, packed):
        c, first = place_of(p)
        ref[c, first : first + slots, :share] = packed.reshape(slots, share, LANES)

    for c in range(chunks):
        loads[2 * c].wait()
        loads[2 * c + 1].wait()
        for p in range(c * group, (c + 1) * group):
            put(kv, p, pack(tn(k[:, lanes(p)], v[:, lanes(p)])))
        if c == 0:
            pl.semaphore_wait(barrier, len(mates) + len(twins))
        send(0, c, kv, kv_in)
    load(q_hbm.at[0], q)
    load(g_hbm.at[0], g)
    load(gain_hbm, gain_ref)

    loads[2 * chunks].wait()
    t = lax.broadcasted_iota(jnp.int32, (2 * GROUP, GROUP), 0) % GROUP
    causal = t >= lax.broadcasted_iota(jnp.int32, (2 * GROUP, GROUP), 1)

    def within(first, last):
        for p in range(pairs * first // 8, pairs * last // 8):
            s = nt(by_head(q[:, lanes(p)]), k[:, lanes(p)])
            s = jnp.where(causal, s, 0.0).astype(BF16)
            scores[p] = s
            q_turned[p] = q[:, lanes(p)].T
            attn[:, lanes(p)] = nn(side_by_side(s), by_head(v[:, lanes(p)]))

    ahead = range(half)
    lower = upper == 0
    within(0, 3)
    for c in range(chunks):
        landed(0, c, kv_in)
        cross(0, c, kv_in, lower)
    for c in range(chunks):
        crossed(0, c, lower)
        scan(0, c, kv_in, prefix, ahead)
        send(1, c, prefix, state)
    within(3, 8)
    loads[2 * chunks + 1].wait()
    loads[2 * chunks + 2].wait()

    for p in range(pairs):
        grad_norm[:, lanes(p)] = g[:, lanes(p)].astype(F32) * gain_ref[:, lanes(p)]

    squares = jnp.zeros((GROUP, LANES), F32)
    cross_sum = jnp.zeros((GROUP, LANES), F32)
    for c in range(chunks):
        landed(1, c, state)
        for p in range(c * group, (c + 1) * group):
            a = attn[:, lanes(p)] + nn(q[:, lanes(p)], unpack(pair_of(state, p)))
            attn[:, lanes(p)] = a
            squares += a * a
            cross_sum += a * grad_norm[:, lanes(p)]
    inv = lax.rsqrt(jnp.sum(squares, 1, keepdims=True) / width + 1e-06)
    mean = jnp.sum(cross_sum, 1, keepdims=True) * inv / width
    tile = qd.shape[2] - share
    for c in range(chunks):
        for p in range(c * group, (c + 1) * group):
            normed = attn[:, lanes(p)] * inv
            ga = (inv * (grad_norm[:, lanes(p)] - normed * mean)).astype(BF16)
            grad_attn[:, lanes(p)] = ga
            put(qd, p, pack(nn(q_turned[p], ga)))
            gf = g[:, lanes(p)].astype(F32)
            gain_tile = jnp.sum((gf * normed).reshape(GROUP // tile, tile, LANES), 0)
            for j in range(p * half // pairs, (p + 1) * half // pairs):
                qd[chunks - 1, j, share:] = gain_tile
        send(2, c, qd, qd_in, tile)

    def after(first, last):
        for p in range(pairs * first // 8, pairs * last // 8):
            normed = attn[:, lanes(p)] * inv
            o_out[:, lanes(p)] = (normed * gain_ref[:, lanes(p)]).astype(BF16)
            ga = grad_attn[:, lanes(p)]
            ga2 = by_head(ga)
            ds = jnp.where(causal, nt(ga2, v[:, lanes(p)]), 0.0).astype(BF16)
            gq = nn(side_by_side(ds), by_head(k[:, lanes(p)]))
            gq = gq + nt(ga, unpack(pair_of(state, p)))
            gq_out[:, lanes(p)] = gq.astype(BF16)
            gk_part[:, lanes(p)] = tn(ds, by_head(q[:, lanes(p)]))
            gv_part[:, lanes(p)] = tn(scores[p], ga2)

    back = range(half - 1, -1, -1)
    raised = upper == 1
    after(0, 2)
    for c in range(chunks):
        landed(2, c, qd_in, tile)
        cross(1, c, qd_in, raised)
    slot = 2 * row + upper
    gains[slot] = functools.reduce(jnp.add, [qd_in[chunks - 1, j, share:] for j in range(half)])
    for d, c in twins:
        pltpu.make_async_remote_copy(
            src_ref=gains.at[slot],
            dst_ref=gains.at[slot],
            send_sem=gain_send,
            recv_sem=gain_recv,
            device_id={"dp": d, "ctx": c},
            device_id_type=MESH,
        ).start()
    rest = gains.at[pl.ds(0, len(twins))]
    for c in range(chunks):
        crossed(1, c, raised)
        scan(1, c, qd_in, suffix, back)
        if c == chunks - 1:
            pltpu.make_async_copy(rest, rest, gain_recv).wait()
            gain_sum = functools.reduce(jnp.add, [gains[j] for j in range(2 * ndp)])
            for j in range(half):
                suffix[c, j, share:] = gain_sum
        send(3, c, suffix, later, tile)
    after(2, 8)

    pltpu.make_async_copy(rest, rest, gain_send).wait()
    left(0, kv)
    left(1, prefix)
    left(2, qd, tile)
    left(3, suffix, tile)
    for c in range(chunks):
        landed(3, c, later, tile)


def last_kernel(
    k, v, o, gq, gk_part, gv_part, later,
    out_hbm, gq_hbm, gk_hbm, gv_hbm, gg_hbm, gk_out, gv_out, gg, sems,
):
    stores = []

    def store(src, dst):
        stores.append(pltpu.make_async_copy(src, dst, sems.at[len(stores)]))
        stores[-1].start()

    store(o, out_hbm.at[0])
    store(gq, gq_hbm.at[0])
    width = k.shape[1]
    pairs = width // LANES
    chunks, half = later.shape[:2]
    group = pairs // chunks
    share = group * HEAD_DIM // half
    for p in range(pairs):
        gg[p : p + 1] = jnp.sum(later[chunks - 1, p * half // pairs, share:], 0, keepdims=True)
    store(gg, gg_hbm)
    for p in range(pairs):
        lanes = slice(p * LANES, (p + 1) * LANES)
        first = p % group * HEAD_DIM // share
        low = later[p // group, first : first + HEAD_DIM // share, :share]
        low = unpack(low.reshape(HEAD_DIM, LANES))
        gk_out[:, lanes] = (gk_part[:, lanes] + nt(v[:, lanes], low)).astype(BF16)
        gv_out[:, lanes] = (gv_part[:, lanes] + nn(k[:, lanes], low)).astype(BF16)
        if (p + 1) % (pairs // 2) == 0:
            done = slice((p + 1 - pairs // 2) * LANES, (p + 1) * LANES)
            store(gk_out.at[:, done], gk_hbm.at[0, :, done])
            store(gv_out.at[:, done], gv_hbm.at[0, :, done])
    for copy in stores:
        copy.wait()


def pinned(x):
    return pltpu.with_memory_space_constraint(x, pltpu.HBM)


def per_device(n, ndp, queries, keys, values, gain, grad_out):
    rows, width = queries.shape[1:]
    pairs = width // LANES
    half = n // 2
    chunks = 4 if pairs * HEAD_DIM // half >= 32 else 2
    share = pairs // chunks * HEAD_DIM // half
    gain_rows = width // LANES
    flat = jax.ShapeDtypeStruct((1, rows, width), BF16)
    low_out = jax.ShapeDtypeStruct((rows, width), BF16)
    full_out = jax.ShapeDtypeStruct((rows, width), F32)
    gain_out = jax.ShapeDtypeStruct((gain_rows, LANES), F32)
    hbm = pl.BlockSpec(memory_space=pltpu.HBM)
    vmem = pl.BlockSpec(memory_space=pltpu.VMEM)
    low = pltpu.VMEM((rows, width), BF16)
    full = pltpu.VMEM((rows, width), F32)
    part = pltpu.VMEM((chunks, half, share, LANES), F32)
    tile = 8
    wide = pltpu.VMEM((chunks, half, share + tile, LANES), F32)
    pair = pltpu.VMEM((2, chunks, share, LANES), F32)
    dma = pltpu.SemaphoreType.DMA
    k, v, o, gq, gk, gv, later = pl.pallas_call(
        functools.partial(scan_kernel, n, ndp),
        out_shape=[low_out] * 4
        + [full_out] * 2
        + [jax.ShapeDtypeStruct((chunks, half, share + tile, LANES), F32)],
        in_specs=[hbm] * 5,
        out_specs=[vmem] * 7,
        scratch_shapes=[low, low, pltpu.VMEM((1, width), F32), full, low]
        + [pltpu.VMEM((pairs, 2 * GROUP, GROUP), BF16), pltpu.VMEM((pairs, LANES, GROUP), BF16)]
        + [full]
        + [part] * 4
        + [wide] * 3
        + [pair, pair, pltpu.VMEM((2 * ndp, tile, LANES), F32)]
        + [dma((2 * chunks + 3,))] + [dma((4, chunks))] * 2 + [dma((2, chunks))] * 2 + [dma, dma],
        compiler_params=pltpu.CompilerParams(
            collective_id=0, has_side_effects=True, vmem_limit_bytes=32 * 2**20
        ),
        name="linear_attention",
    )(*(pinned(x) for x in (queries, keys, values, gain.reshape(1, width), grad_out)))
    out, gq, gk, gv, gg = pl.pallas_call(
        last_kernel,
        out_shape=[flat] * 4 + [gain_out],
        in_specs=[vmem] * 7,
        out_specs=[hbm] * 5,
        scratch_shapes=[low, low, pltpu.VMEM((gain_rows, LANES), F32), dma((7,))],
        compiler_params=pltpu.CompilerParams(vmem_limit_bytes=32 * 2**20),
        name="last_products",
    )(k, v, o, gq, gk, gv, later)
    return out, gq, gk, gv, gg.reshape(width)


def solution(mesh):
    spec = P("dp", "ctx", None)
    return jax.shard_map(
        functools.partial(per_device, mesh.shape["ctx"], mesh.shape["dp"]),
        mesh=mesh,
        in_specs=(spec, spec, spec, P(), spec),
        out_specs=(spec, spec, spec, spec, P()),
        check_vma=False,
    )
```
